32 devices in a mesh: seq: 16 (over z, y, x), dp: 2 (over core).
Axes of the slice: x: 2, y: 2, z: 4, core: 2. Of those that a mesh axis runs over, the one named last changes fastest.
Arguments:
- query_proj: bfloat16 [10240, 1024], P(('dp', 'seq')), parts along dimension 0, may hold values from -8 to 8
- key_proj: bfloat16 [10240, 1024], P(('dp', 'seq')), parts along dimension 0, may hold values from -8 to 8
- value_proj: bfloat16 [10240, 1024], P(('dp', 'seq')), parts along dimension 0, may hold values from -6 to 6
- residual_in: bfloat16 [10240, 1024], P(('dp', 'seq')), parts along dimension 0, may hold values from -6 to 6
- utter_lengths: int32 [32], P('dp'), parts along dimension 0, may hold values from 1 to 640, 5120 in all
- depth_kernel: float32 [31, 1024], replicated, may hold values from -1 to 1
- norm_gain: float32 [1024], replicated, may hold values from 0.5 to 1.5
- norm_shift: float32 [1024], replicated, may hold values from -3 to 3
Outputs:
- block_out: bfloat16 [10240, 1024], P(('dp', 'seq')), parts along dimension 0
The draws below stay inside these ranges and needn't reach their ends.
There are 2 independent parts, one for each index of `dp`. The reference program is written for one: setup_inputs(seed, part) draws one part's arguments, and reference() takes and returns one part's arrays. A program takes and returns all parts, laid end to end along the dimension named above; an argument that names none is the same for every part. Nothing has to cross between parts.
Inputs may be any that keep to these rules, and one draw needn't show every extreme that they name: `utter_lengths`: the lengths sum to 5120; the largest is exactly 640.
All inputs are finite; a program needn't handle non-finite values.
Results may differ from the reference program's by a relative error of at most 0.005.
Values may be sent and summed in bfloat16 or wider, within the bound.
No kernel may reach another device: no remote copies, remote signals or barrier semaphores. Data moves between devices by JAX's collectives and lax.ppermute only.
A program may use at most 64 MiB of HBM per device.

```python
import math
import jax
import jax.numpy as jnp
import numpy as np
from jax import lax

HD = 64
D = 1024
KERNEL = 31
ROWS = 320
FRAMES = 5120
UTTS = 16
N_SEQ = 16


def shared_pair(key):
    query_base = jnp.clip(jax.random.normal(jax.random.fold_in(key, 11), (FRAMES, D), jnp.float32), -8.0, 8.0)
    key_base = jnp.clip(jax.random.normal(jax.random.fold_in(key, 12), (FRAMES, D), jnp.float32), -8.0, 8.0)
    return (query_base, key_base)


def draw_query_proj(key, part):
    return shared_pair(key)[0].astype(jnp.bfloat16)


def draw_key_proj(key, part):
    return shared_pair(key)[1].astype(jnp.bfloat16)


def block_scale(key, shape, cuts, low, top_value):
    def one(axis_at, shards_of):
        draws = jax.random.uniform(jax.random.fold_in(jax.random.fold_in(key, 6), axis_at), (shards_of,), jnp.float32, low / len(cuts), top_value / len(cuts))
        return jnp.repeat(jnp.exp(draws), shape[axis_at] // shards_of).reshape((-1,) + (1,) * (len(shape) - axis_at - 1))

    gain = one(*cuts[0])
    for cut in cuts[1:]:
        gain = gain * one(*cut)
    return gain


def length_profile(amount, total, most, slope):
    portions = [(1 << 20) // math.isqrt(rank ** slope) + 1 for rank in range(2, amount + 1)]
    rest, given = total - most - (amount - 1), [1] * (amount - 1)
    while rest > 0:
        free = [i for i in range(amount - 1) if given[i] < most]
        pool, remaining = sum([portions[i] for i in free]), rest
        for i in free:
            extra = min(most - given[i], max(1, remaining * portions[i] // pool), rest)
            given[i] = given[i] + extra
            rest = rest - extra
    return np.array([most] + given)


def ragged(rng, amount, total, most, lean):
    if amount == 2:
        one = jax.random.randint(rng, (), max(1, total - most), min(most, total - 1) + 1)
        return jnp.stack([one, total - one])
    tallies = jnp.asarray(length_profile(amount, total, most, lean), jnp.int32)
    twos = (amount - 1) // 2
    donor, receiver = tallies[1:1 + 2 * twos:2], tallies[2:2 + 2 * twos:2]
    room = jnp.minimum(donor - 1, most - receiver)
    passed = jax.random.randint(jax.random.fold_in(rng, 1), (twos,), 0, 1 << 20) % (room + 1)
    tallies = tallies.at[1:1 + 2 * twos:2].set(donor - passed).at[2:2 + 2 * twos:2].set(receiver + passed)
    return tallies[jax.random.permutation(jax.random.fold_in(rng, 2), amount)]


def normal_values(own_key, dims, deviation, bound, shards=(), held_as=jnp.bfloat16):
    drawn = deviation * jax.random.normal(own_key, dims, jnp.float32)
    if shards:
        drawn = drawn * block_scale(own_key, dims, shards, -0.22, 0.18)
    return jnp.clip(drawn, -bound, bound).astype(held_as)


def setup_inputs(seed: int = 0, part: int = 0) -> dict:
    key_of = jax.random.split(jax.random.key(seed), 9)
    part_splits = jax.random.split(jax.random.fold_in(key_of[8], part), 9)
    return {
        "query_proj": draw_query_proj(jax.random.fold_in(jax.random.fold_in(key_of[8], part), 71), part),
        "key_proj": draw_key_proj(jax.random.fold_in(jax.random.fold_in(key_of[8], part), 71), part),
        "value_proj": normal_values(part_splits[2], (FRAMES, D), 1.0, 6.0, ((0, 16),)),
        "residual_in": normal_values(part_splits[3], (FRAMES, D), 1.0, 6.0, ((0, 16),)),
        "utter_lengths": ragged(part_splits[4], UTTS, FRAMES, 2 * ROWS, 1).astype(jnp.int32),
        "depth_kernel": normal_values(key_of[5], (KERNEL, D), KERNEL ** -0.5, 1.0, (), jnp.float32),
        "norm_gain": jnp.clip(1.0 + 0.1 * jax.random.normal(key_of[6], (D,), jnp.float32), 0.5, 1.5),
        "norm_shift": normal_values(key_of[7], (D,), 0.5, 3.0, (), jnp.float32),
    }


def utterance_ids(positions, utt_ends, frames_all):
    counted = lax.optimization_barrier(jnp.sum((utt_ends[None, :] <= positions[:, None]).astype(jnp.int32), axis=1))
    inside = (positions >= 0) & (positions < frames_all)
    return jnp.where(inside, counted, -1).astype(jnp.int32)

def attend(query_rows, query_pos, key_rows, value_rows, key_pos, utt_ends, frames_all):
    query_utt = utterance_ids(query_pos, utt_ends, frames_all)
    key_utt = utterance_ids(key_pos, utt_ends, frames_all)
    same_utt = (query_utt[:, None] == key_utt[None, :])[None]
    score_scale = HD ** (-0.5)
    group_width = 2 * HD
    pieces = []
    for first_col in range(0, query_rows.shape[1], group_width):
        query_group = query_rows[:, first_col:first_col + group_width].reshape(-1, 2, HD).astype(jnp.float32)
        key_group = key_rows[:, first_col:first_col + group_width].reshape(-1, 2, HD).astype(jnp.float32)
        value_group = value_rows[:, first_col:first_col + group_width].reshape(-1, 2, HD).astype(jnp.float32)
        scores = jnp.einsum('qhd,khd->hqk', query_group, key_group) * score_scale
        scores = jnp.where(same_utt, scores, jnp.float32(-1e+30))
        row_max = lax.optimization_barrier(jnp.max(scores, axis=-1, keepdims=True))
        probs = jnp.where(same_utt, jnp.exp(scores - row_max), jnp.float32(0.0))
        denom = lax.optimization_barrier(jnp.sum(probs, axis=-1))
        weights = probs.astype(jnp.bfloat16).astype(jnp.float32)
        context = jnp.einsum('hqk,khd->qhd', weights, value_group) / denom.T[:, :, None]
        pieces.append(context.reshape(context.shape[0], group_width))
    return jnp.concatenate(pieces, axis=1)

def reference(query_proj, key_proj, value_proj, residual_in, utter_lengths, depth_kernel, norm_gain, norm_shift):
    utt_ends = jnp.cumsum(utter_lengths).astype(jnp.int32)
    margin = 2 * ROWS
    key_padded = jnp.pad(key_proj, ((margin, margin), (0, 0)))
    value_padded = jnp.pad(value_proj, ((margin, margin), (0, 0)))

    def one_block(block_index):
        first_row = block_index * ROWS
        query_rows = lax.dynamic_slice_in_dim(query_proj, first_row, ROWS, 0)
        key_rows = lax.dynamic_slice_in_dim(key_padded, first_row, 5 * ROWS, 0)
        value_rows = lax.dynamic_slice_in_dim(value_padded, first_row, 5 * ROWS, 0)
        query_pos = first_row + jnp.arange(ROWS, dtype=jnp.int32)
        key_pos = first_row - margin + jnp.arange(5 * ROWS, dtype=jnp.int32)
        return attend(query_rows, query_pos, key_rows, value_rows, key_pos, utt_ends, FRAMES)
    context = lax.map(one_block, jnp.arange(N_SEQ, dtype=jnp.int32)).reshape(FRAMES, D)
    mixed = (residual_in.astype(jnp.float32) + context).astype(jnp.bfloat16)
    half_width = (KERNEL - 1) // 2
    mixed_padded = jnp.pad(mixed, ((half_width, half_width), (0, 0)))
    own_utt = utterance_ids(jnp.arange(FRAMES, dtype=jnp.int32), utt_ends, FRAMES)
    padded_utt = utterance_ids(jnp.arange(FRAMES + 2 * half_width, dtype=jnp.int32) - half_width, utt_ends, FRAMES)
    conv_sum = jnp.zeros((FRAMES, D), jnp.float32)
    for tap in range(KERNEL):
        same_utt = padded_utt[tap:tap + FRAMES] == own_utt
        term = mixed_padded[tap:tap + FRAMES].astype(jnp.float32) * depth_kernel[tap][None, :]
        conv_sum = conv_sum + jnp.where(same_utt[:, None], term, jnp.float32(0.0))
    mean_val = lax.optimization_barrier(jnp.mean(conv_sum, axis=1, keepdims=True))
    centred = conv_sum - mean_val
    var_val = lax.optimization_barrier(jnp.mean(centred * centred, axis=1, keepdims=True))
    normed = centred / jnp.sqrt(var_val + 1e-05) * norm_gain[None, :] + norm_shift[None, :]
    return (mixed.astype(jnp.float32) + normed * jax.nn.sigmoid(normed)).astype(jnp.bfloat16)
```

```python
import functools

import jax
import jax.numpy as jnp
from jax import lax
from jax.experimental import pallas as pl
from jax.experimental.pallas import tpu as pltpu
from jax.sharding import PartitionSpec as P

HD = 64
LANES = 128
GROUP = 4
EDGE = 16
SAME = 2048.0
MIB = 1 << 20

ANY = pl.BlockSpec(memory_space=pl.ANY)
VMEM = pl.BlockSpec(memory_space=pltpu.VMEM)
SMEM = pl.BlockSpec(memory_space=pltpu.SMEM)


def utterance_of(positions, ends):
    return jnp.sum((ends[None, :] <= positions[:, None]).astype(jnp.int32), axis=1)


def split_kernel(cols, which, *refs):
    n_in = len(refs) - GROUP - 1
    srcs, outs, sem = refs[:n_in], refs[n_in:-1], refs[-1]
    copies = []
    for m in range(GROUP):
        first = pl.multiple_of(which[m] * cols, LANES)
        for i, src in enumerate(srcs):
            copies.append(
                pltpu.make_async_copy(
                    src.at[:, pl.ds(first, cols)],
                    outs[m].at[:, pl.ds(i * cols, cols)],
                    sem.at[m * n_in + i],
                )
            )
    for copy in copies:
        copy.start()
    for copy in copies:
        copy.wait()


def split_columns(which, *arrays):
    rows, width = arrays[0].shape
    cols = width // GROUP
    shape = jax.ShapeDtypeStruct((rows, cols * len(arrays)), arrays[0].dtype)
    return pl.pallas_call(
        functools.partial(split_kernel, cols),
        out_shape=[shape] * GROUP,
        in_specs=[SMEM] + [ANY] * len(arrays),
        out_specs=[ANY] * GROUP,
        scratch_shapes=[pltpu.SemaphoreType.DMA((GROUP * len(arrays),))],
        name="split_columns",
    )(which, *arrays)


def attend_kernel(rows, q_rows, widths, meta, place, starts, ends, *refs):
    q_in, kv_in, outs = refs[:GROUP], refs[GROUP : 3 * GROUP], refs[3 * GROUP : 4 * GROUP]
    q_buf, kv_buf, oh_buf, ctx_buf, q_sem, kv_sem, out_sem = refs[4 * GROUP :]
    heads_cols = q_buf.shape[2]
    copies = []
    for i, src in enumerate(kv_in):
        at = pl.multiple_of(place[i] * rows, 16)
        copies.append(pltpu.make_async_copy(src, kv_buf.at[pl.ds(at, rows), :], kv_sem.at[i]))
    for m, src in enumerate(q_in):
        copies.append(pltpu.make_async_copy(src, q_buf.at[m], q_sem.at[m]))
    for copy in copies:
        copy.start()

    def one_hot(first, n, value):
        frame = first + lax.broadcasted_iota(jnp.int32, (n, starts.shape[1]), 0)
        inside = (frame >= starts[...]) & (frame < ends[...])
        return jnp.where(inside, jnp.float32(value), jnp.float32(0.0)).astype(jnp.bfloat16)

    step = rows // 2

    @pl.loop(0, kv_buf.shape[0] // step)
    def _(i):
        at = pl.multiple_of(i * step, 16)
        oh_buf[pl.ds(at, step), :] = one_hot(meta[0] + at, step, 1.0)

    for copy in copies:
        copy.wait()

    blocks = q_buf.shape[1] // q_rows
    lane = lax.broadcasted_iota(jnp.int32, (1, LANES), 1)
    scale = HD**-0.5
    halves = [
        jnp.where(lane // HD == h, jnp.float32(scale), jnp.float32(0.0)).astype(jnp.bfloat16)
        for h in range(2)
    ]

    def block(m, b, width):
        t = m * blocks + b
        low = pl.multiple_of(meta[1 + GROUP + t], 16)
        first = pl.multiple_of(b * q_rows, 16)
        oh_q = one_hot(meta[1 + m] + first, q_rows, SAME)
        oh_k = oh_buf[pl.ds(low, width), :]
        ones = jnp.ones((width, LANES), jnp.bfloat16)
        for pair in range(heads_cols // LANES):
            cols = slice(pair * LANES, (pair + 1) * LANES)
            v_cols = slice(heads_cols + pair * LANES, heads_cols + (pair + 1) * LANES)
            q = q_buf[m, pl.ds(first, q_rows), cols]
            k = jnp.concatenate([kv_buf[pl.ds(low, width), cols], oh_k], axis=1)
            v = jnp.concatenate([kv_buf[pl.ds(low, width), v_cols], ones], axis=1)
            got = []
            for h in range(2):
                q_h = jnp.concatenate([q * halves[h], oh_q], axis=1)
                s = lax.dot_general(
                    q_h, k, (((1,), (1,)), ((), ())), preferred_element_type=jnp.float32
                )
                p = jnp.exp(s - jnp.max(s, axis=1, keepdims=True)).astype(jnp.bfloat16)
                o = jnp.dot(p, v, preferred_element_type=jnp.float32)
                got.append(o[:, :LANES] / o[:, LANES:])
            ctx = jnp.where(lane < HD, got[0], got[1]).astype(jnp.bfloat16)
            ctx_buf[m, pl.ds(first, q_rows), cols] = ctx

    @pl.loop(0, GROUP * blocks)
    def _(t):
        m, b = t // blocks, t % blocks
        need = meta[1 + GROUP + GROUP * blocks + t]
        below = 0
        for width in widths:

            @pl.when((need > below) & (need <= width))
            def _(width=width):
                block(m, b, width)

            below = width

    copies = [
        pltpu.make_async_copy(ctx_buf.at[m], outs[m], out_sem.at[m]) for m in range(GROUP)
    ]
    for copy in copies:
        copy.start()
    for copy in copies:
        copy.wait()


def attend(rows, q_rows, widths, meta, place, starts, ends, q_parts, kv_parts):
    ext, cols = q_parts[0].shape
    keys = 2 * GROUP * rows
    shape = jax.ShapeDtypeStruct((ext, cols), jnp.bfloat16)
    dma = pltpu.SemaphoreType.DMA
    return pl.pallas_call(
        functools.partial(attend_kernel, rows, q_rows, widths),
        out_shape=[shape] * GROUP,
        in_specs=[SMEM, SMEM, VMEM, VMEM] + [ANY] * (3 * GROUP),
        out_specs=[ANY] * GROUP,
        scratch_shapes=[
            pltpu.VMEM((GROUP, ext, cols), jnp.bfloat16),
            pltpu.VMEM((keys, 2 * cols), jnp.bfloat16),
            pltpu.VMEM((keys, starts.shape[1]), jnp.bfloat16),
            pltpu.VMEM((GROUP, ext, cols), jnp.bfloat16),
            dma((GROUP,)),
            dma((2 * GROUP,)),
            dma((GROUP,)),
        ],
        compiler_params=pltpu.CompilerParams(vmem_limit_bytes=40 * MIB),
        name="attend",
    )(meta, place, starts, ends, *q_parts, *kv_parts)


def finish_kernel(block_rows, taps, meta, starts, ends, *refs):
    ctx_in = refs[:GROUP]
    res, res_before, res_after, kernel, gain, shift, out = refs[GROUP : GROUP + 7]
    mixed, window, conv = refs[GROUP + 7 :]
    rows, width = res.shape
    tiles = width // LANES
    per = tiles // GROUP
    half = taps // 2
    n_blocks = rows // block_rows
    for m in range(GROUP):
        for t in range(per):
            cols = slice(t * LANES, (t + 1) * LANES)
            mixed[meta[1 + m] * per + t] = ctx_in[m][:, cols].astype(jnp.float32)
    for t in range(tiles):
        cols = slice(t * LANES, (t + 1) * LANES)
        for first, part in ((0, res_before), (EDGE, res), (EDGE + rows, res_after)):
            at = slice(first, first + part.shape[0])
            total = part[:, cols].astype(jnp.float32) + mixed[t, at, :]
            mixed[t, at, :] = total.astype(jnp.bfloat16).astype(jnp.float32)

    span = block_rows + 2 * EDGE

    @pl.loop(0, n_blocks)
    def _(b):
        top = pl.multiple_of(b * block_rows, 8)
        first_frame = meta[0] + top
        around = first_frame - EDGE + lax.broadcasted_iota(jnp.int32, (span, LANES), 0)
        frame = first_frame + lax.broadcasted_iota(jnp.int32, (block_rows, LANES), 0)

        @pl.loop(meta[1 + GROUP + b], meta[1 + GROUP + n_blocks + b] + 1)
        def _(u):
            low, high = starts[u], ends[u]
            kept = (around >= low) & (around < high)
            mine = (frame >= low) & (frame < high)
            for t in range(tiles):
                window[t] = jnp.where(kept, mixed[t, pl.ds(top, span), :], jnp.float32(0.0))
            for t in range(tiles):
                cols = slice(t * LANES, (t + 1) * LANES)
                total = jnp.zeros((block_rows, LANES), jnp.float32)
                for tap in range(taps):
                    at = tap + EDGE - half
                    total = total + window[t, at : at + block_rows, :] * kernel[tap : tap + 1, cols]
                conv[t] = jnp.where(mine, total, conv[t])

        values = [conv[t] for t in range(tiles)]
        mean = jnp.sum(sum(values), axis=1, keepdims=True) / width
        centred = [x - mean for x in values]
        var = jnp.sum(sum([x * x for x in centred]), axis=1, keepdims=True) / width
        inverse = 1.0 / jnp.sqrt(var + 1e-05)
        for t in range(tiles):
            cols = slice(t * LANES, (t + 1) * LANES)
            normed = centred[t] * inverse * gain[:, cols] + shift[:, cols]
            gated = normed * jax.nn.sigmoid(normed)
            own = mixed[t, pl.ds(pl.multiple_of(top + EDGE, 8), block_rows), :]
            out[pl.ds(pl.multiple_of(top, 16), block_rows), cols] = (own + gated).astype(
                jnp.bfloat16
            )


def finish(block_rows, meta, starts, ends, ctx_parts, res, before, after, kernel, gain, shift):
    rows, width = res.shape
    tiles = width // LANES
    return pl.pallas_call(
        functools.partial(finish_kernel, block_rows, kernel.shape[0]),
        out_shape=jax.ShapeDtypeStruct((rows, width), jnp.bfloat16),
        in_specs=[SMEM, SMEM, SMEM] + [VMEM] * (GROUP + 6),
        out_specs=VMEM,
        scratch_shapes=[
            pltpu.VMEM((tiles, rows + 2 * EDGE, LANES), jnp.float32),
            pltpu.VMEM((tiles, block_rows + 2 * EDGE, LANES), jnp.float32),
            pltpu.VMEM((tiles, block_rows, LANES), jnp.float32),
        ],
        compiler_params=pltpu.CompilerParams(vmem_limit_bytes=40 * MIB),
        name="finish",
    )(meta, starts, ends, *ctx_parts, res, before, after, kernel, gain, shift)


def local(query, key, value, residual, lengths, depth_kernel, gain, shift):
    rows, width = query.shape
    peers = lax.axis_size("seq")
    frames = rows * peers
    me = lax.axis_index("seq")
    member = me % GROUP
    others = jnp.arange(GROUP, dtype=jnp.int32) ^ member
    halo = 2 * rows
    base = (me - member) * rows
    key_base = base - halo
    keys = GROUP * rows + 2 * halo

    def swap(array, m):
        return lax.ppermute(array, "seq", [(i, i ^ m) for i in range(peers)])

    def move(array, by):
        pairs = [(i, i + by(i)) for i in range(peers)]
        return lax.ppermute(array, "seq", [(i, j) for i, j in pairs if 0 <= j < peers])

    near = lambda i: -GROUP if i % GROUP < GROUP // 2 else GROUP
    far = lambda i: -near(i)

    kv = split_columns(others, key, value)
    kv_group = [kv[0]] + [swap(kv[m], m) for m in range(1, GROUP)]
    kv_halo = [move(kv_group[m], near if m < 2 else far) for m in range(GROUP)]

    last = jnp.concatenate([query[rows - EDGE :], residual[rows - EDGE :]], axis=1)
    initial = jnp.concatenate([query[:EDGE], residual[:EDGE]], axis=1)
    before = move(last, lambda i: 1)
    after = move(initial, lambda i: -1)
    query_ext = jnp.concatenate([before[:, :width], query, after[:, :width]], axis=0)
    q_out = split_columns(others, query_ext)
    q_group = [q_out[0]] + [swap(q_out[m], m) for m in range(1, GROUP)]

    ends = jnp.cumsum(lengths).astype(jnp.int32)
    starts = ends - lengths
    n_utts = lengths.shape[0]
    q_rows = (rows + 2 * EDGE) // 2
    halves = jnp.arange(2, dtype=jnp.int32)
    block_first = base + others[:, None] * rows
    first_own = jnp.where(halves == 0, 0, q_rows - EDGE)
    last_own = jnp.where(halves == 0, q_rows - EDGE - 1, rows - 1)
    first_utt = utterance_of((block_first + first_own).reshape(-1), ends)
    last_utt = utterance_of((block_first + last_own).reshape(-1), ends)
    low = (jnp.maximum(starts[first_utt] - key_base, 0) // 16) * 16
    high = jnp.minimum(ends[last_utt] - key_base, keys)
    need = high - low
    most = -(-(q_rows + 2 * halo + 16) // LANES) * LANES
    widths = sorted({min(w, most) for w in (256, 512, 768, 1024, most)})
    taken = functools.reduce(
        lambda later, w: jnp.where(need <= w, w, later), widths[::-1], jnp.full_like(need, most)
    )
    low = jnp.minimum(low, keys - taken)
    meta = jnp.concatenate(
        [key_base[None], base + others * rows - EDGE, low, need]
    ).astype(jnp.int32)
    at_group = others + GROUP // 2
    at_halo = jnp.where(others < GROUP // 2, others + 3 * GROUP // 2, others - GROUP // 2)
    place = jnp.concatenate([at_group, at_halo]).astype(jnp.int32)
    pad = -n_utts % LANES
    lane_starts = jnp.pad(starts, (0, pad))[None, :]
    lane_ends = jnp.pad(ends, (0, pad))[None, :]
    ctx = attend(
        rows, q_rows, widths, meta, place, lane_starts, lane_ends, q_group, kv_group + kv_halo
    )
    ctx_group = [ctx[0]] + [swap(ctx[m], m) for m in range(1, GROUP)]

    block_rows = 32
    n_blocks = rows // block_rows
    block_tops = me * rows + jnp.arange(n_blocks, dtype=jnp.int32) * block_rows
    meta_out = jnp.concatenate(
        [
            (me * rows)[None],
            others,
            utterance_of(block_tops, ends),
            utterance_of(block_tops + block_rows - 1, ends),
        ]
    ).astype(jnp.int32)
    return finish(
        block_rows,
        meta_out,
        starts,
        ends,
        ctx_group,
        residual,
        before[:, width:],
        after[:, width:],
        depth_kernel,
        gain[None, :],
        shift[None, :],
    )


def solution(mesh):
    return jax.shard_map(
        local,
        mesh=mesh,
        in_specs=(
            P(("dp", "seq"), None),
            P(("dp", "seq"), None),
            P(("dp", "seq"), None),
            P(("dp", "seq"), None),
            P("dp"),
            P(),
            P(),
            P(),
        ),
        out_specs=P(("dp", "seq"), None),
        check_vma=False,
    )
```

```python
import functools

import jax
import jax.numpy as jnp
from jax import lax
from jax.experimental import pallas as pl
from jax.experimental.pallas import tpu as pltpu
from jax.sharding import PartitionSpec as P

HD = 64
LANES = 128
GROUP = 4
EDGE = 16
SAME = 2048.0
MIB = 1 << 20

ANY = pl.BlockSpec(memory_space=pl.ANY)
VMEM = pl.BlockSpec(memory_space=pltpu.VMEM)
SMEM = pl.BlockSpec(memory_space=pltpu.SMEM)


def utterance_of(positions, ends):
    return jnp.sum((ends[None, :] <= positions[:, None]).astype(jnp.int32), axis=1)


def split_kernel(cols, which, *refs):
    srcs, outs = refs[:-GROUP], refs[-GROUP:]
    for m in range(GROUP):
        first = pl.multiple_of(which[m] * cols, LANES)
        for i, src in enumerate(srcs):
            outs[m][:, i * cols : (i + 1) * cols] = src[:, pl.ds(first, cols)]


def split_columns(which, *arrays):
    rows, width = arrays[0].shape
    cols = width // GROUP
    shape = jax.ShapeDtypeStruct((rows, cols * len(arrays)), arrays[0].dtype)
    return pl.pallas_call(
        functools.partial(split_kernel, cols),
        out_shape=[shape] * GROUP,
        in_specs=[SMEM] + [VMEM] * len(arrays),
        out_specs=[VMEM] * GROUP,
        compiler_params=pltpu.CompilerParams(vmem_limit_bytes=16 * MIB),
        name="split_columns",
    )(which, *arrays)


def attend_kernel(rows, q_rows, widths, meta, place, starts, ends, *refs):
    q_in, kv_in, outs = refs[:GROUP], refs[GROUP : 3 * GROUP], refs[3 * GROUP : 4 * GROUP]
    q_buf, kv_buf, oh_buf, ctx_buf, q_sem, kv_sem, out_sem = refs[4 * GROUP :]
    heads_cols = q_buf.shape[2]
    copies = []
    for i, src in enumerate(kv_in):
        at = pl.multiple_of(place[i] * rows, 16)
        copies.append(pltpu.make_async_copy(src, kv_buf.at[pl.ds(at, rows), :], kv_sem.at[i]))
    for m, src in enumerate(q_in):
        copies.append(pltpu.make_async_copy(src, q_buf.at[m], q_sem.at[m]))
    for copy in copies:
        copy.start()

    def one_hot(first, n, value):
        frame = first + lax.broadcasted_iota(jnp.int32, (n, starts.shape[1]), 0)
        inside = (frame >= starts[...]) & (frame < ends[...])
        return jnp.where(inside, jnp.float32(value), jnp.float32(0.0)).astype(jnp.bfloat16)

    step = rows // 2

    @pl.loop(0, kv_buf.shape[0] // step)
    def _(i):
        at = pl.multiple_of(i * step, 16)
        oh_buf[pl.ds(at, step), :] = one_hot(meta[0] + at, step, 1.0)

    for copy in copies:
        copy.wait()

    blocks = q_buf.shape[1] // q_rows
    lane = lax.broadcasted_iota(jnp.int32, (1, LANES), 1)
    scale = HD**-0.5
    halves = [
        jnp.where(lane // HD == h, jnp.float32(scale), jnp.float32(0.0)).astype(jnp.bfloat16)
        for h in range(2)
    ]

    def block(m, b, width):
        t = m * blocks + b
        low = pl.multiple_of(meta[1 + GROUP + t], 16)
        first = pl.multiple_of(b * q_rows, 16)
        oh_q = one_hot(meta[1 + m] + first, q_rows, SAME)
        oh_k = oh_buf[pl.ds(low, width), :]
        ones = jnp.ones((width, LANES), jnp.bfloat16)
        for pair in range(heads_cols // LANES):
            cols = slice(pair * LANES, (pair + 1) * LANES)
            v_cols = slice(heads_cols + pair * LANES, heads_cols + (pair + 1) * LANES)
            q = q_buf[m, pl.ds(first, q_rows), cols]
            k = jnp.concatenate([kv_buf[pl.ds(low, width), cols], oh_k], axis=1)
            v = jnp.concatenate([kv_buf[pl.ds(low, width), v_cols], ones], axis=1)
            got = []
            for h in range(2):
                q_h = jnp.concatenate([q * halves[h], oh_q], axis=1)
                s = lax.dot_general(
                    q_h, k, (((1,), (1,)), ((), ())), preferred_element_type=jnp.float32
                )
                p = jnp.exp(s - jnp.max(s, axis=1, keepdims=True)).astype(jnp.bfloat16)
                o = jnp.dot(p, v, preferred_element_type=jnp.float32)
                got.append(o[:, :LANES] / o[:, LANES:])
            ctx = jnp.where(lane < HD, got[0], got[1]).astype(jnp.bfloat16)
            ctx_buf[m, pl.ds(first, q_rows), cols] = ctx

    @pl.loop(0, GROUP * blocks)
    def _(t):
        m, b = t // blocks, t % blocks
        need = meta[1 + GROUP + GROUP * blocks + t]
        below = 0
        for width in widths:

            @pl.when((need > below) & (need <= width))
            def _(width=width):
                block(m, b, width)

            below = width

    copies = [
        pltpu.make_async_copy(ctx_buf.at[m], outs[m], out_sem.at[m]) for m in range(GROUP)
    ]
    for copy in copies:
        copy.start()
    for copy in copies:
        copy.wait()


def attend(rows, q_rows, widths, meta, place, starts, ends, q_parts, kv_parts):
    ext, cols = q_parts[0].shape
    keys = 2 * GROUP * rows
    shape = jax.ShapeDtypeStruct((ext, cols), jnp.bfloat16)
    dma = pltpu.SemaphoreType.DMA
    return pl.pallas_call(
        functools.partial(attend_kernel, rows, q_rows, widths),
        out_shape=[shape] * GROUP,
        in_specs=[SMEM, SMEM, VMEM, VMEM] + [ANY] * (3 * GROUP),
        out_specs=[ANY] * GROUP,
        scratch_shapes=[
            pltpu.VMEM((GROUP, ext, cols), jnp.bfloat16),
            pltpu.VMEM((keys, 2 * cols), jnp.bfloat16),
            pltpu.VMEM((keys, starts.shape[1]), jnp.bfloat16),
            pltpu.VMEM((GROUP, ext, cols), jnp.bfloat16),
            dma((GROUP,)),
            dma((2 * GROUP,)),
            dma((GROUP,)),
        ],
        compiler_params=pltpu.CompilerParams(vmem_limit_bytes=40 * MIB),
        name="attend",
    )(meta, place, starts, ends, *q_parts, *kv_parts)


def finish_kernel(block_rows, taps, meta, starts, ends, *refs):
    ctx_in = refs[:GROUP]
    res, res_before, res_after, kernel, gain, shift, out = refs[GROUP : GROUP + 7]
    mixed, window, conv = refs[GROUP + 7 :]
    rows, width = res.shape
    tiles = width // LANES
    per = tiles // GROUP
    half = taps // 2
    n_blocks = rows // block_rows
    for m in range(GROUP):
        for t in range(per):
            cols = slice(t * LANES, (t + 1) * LANES)
            mixed[meta[1 + m] * per + t] = ctx_in[m][:, cols].astype(jnp.float32)
    for t in range(tiles):
        cols = slice(t * LANES, (t + 1) * LANES)
        for first, part in ((0, res_before), (EDGE, res), (EDGE + rows, res_after)):
            at = slice(first, first + part.shape[0])
            total = part[:, cols].astype(jnp.float32) + mixed[t, at, :]
            mixed[t, at, :] = total.astype(jnp.bfloat16).astype(jnp.float32)

    span = block_rows + 2 * EDGE

    @pl.loop(0, n_blocks)
    def _(b):
        top = pl.multiple_of(b * block_rows, 8)
        first_frame = meta[0] + top
        around = first_frame - EDGE + lax.broadcasted_iota(jnp.int32, (span, LANES), 0)
        frame = first_frame + lax.broadcasted_iota(jnp.int32, (block_rows, LANES), 0)

        @pl.loop(meta[1 + GROUP + b], meta[1 + GROUP + n_blocks + b] + 1)
        def _(u):
            low, high = starts[u], ends[u]
            kept = (around >= low) & (around < high)
            mine = (frame >= low) & (frame < high)
            for t in range(tiles):
                window[t] = jnp.where(kept, mixed[t, pl.ds(top, span), :], jnp.float32(0.0))
            for t in range(tiles):
                cols = slice(t * LANES, (t + 1) * LANES)
                total = jnp.zeros((block_rows, LANES), jnp.float32)
                for tap in range(taps):
                    at = tap + EDGE - half
                    total = total + window[t, at : at + block_rows, :] * kernel[tap : tap + 1, cols]
                conv[t] = jnp.where(mine, total, conv[t])

        values = [conv[t] for t in range(tiles)]
        mean = jnp.sum(sum(values), axis=1, keepdims=True) / width
        centred = [x - mean for x in values]
        var = jnp.sum(sum([x * x for x in centred]), axis=1, keepdims=True) / width
        inverse = 1.0 / jnp.sqrt(var + 1e-05)
        for t in range(tiles):
            cols = slice(t * LANES, (t + 1) * LANES)
            normed = centred[t] * inverse * gain[:, cols] + shift[:, cols]
            gated = normed * jax.nn.sigmoid(normed)
            own = mixed[t, pl.ds(pl.multiple_of(top + EDGE, 8), block_rows), :]
            out[pl.ds(pl.multiple_of(top, 16), block_rows), cols] = (own + gated).astype(
                jnp.bfloat16
            )


def finish(block_rows, meta, starts, ends, ctx_parts, res, before, after, kernel, gain, shift):
    rows, width = res.shape
    tiles = width // LANES
    return pl.pallas_call(
        functools.partial(finish_kernel, block_rows, kernel.shape[0]),
        out_shape=jax.ShapeDtypeStruct((rows, width), jnp.bfloat16),
        in_specs=[SMEM, SMEM, SMEM] + [VMEM] * (GROUP + 6),
        out_specs=VMEM,
        scratch_shapes=[
            pltpu.VMEM((tiles, rows + 2 * EDGE, LANES), jnp.float32),
            pltpu.VMEM((tiles, block_rows + 2 * EDGE, LANES), jnp.float32),
            pltpu.VMEM((tiles, block_rows, LANES), jnp.float32),
        ],
        compiler_params=pltpu.CompilerParams(vmem_limit_bytes=40 * MIB),
        name="finish",
    )(meta, starts, ends, *ctx_parts, res, before, after, kernel, gain, shift)


def local(query, key, value, residual, lengths, depth_kernel, gain, shift):
    rows, width = query.shape
    peers = lax.axis_size("seq")
    frames = rows * peers
    me = lax.axis_index("seq")
    member = me % GROUP
    others = jnp.arange(GROUP, dtype=jnp.int32) ^ member
    halo = 2 * rows
    base = (me - member) * rows
    key_base = base - halo
    keys = GROUP * rows + 2 * halo

    def swap(array, m):
        return lax.ppermute(array, "seq", [(i, i ^ m) for i in range(peers)])

    def move(array, by):
        pairs = [(i, i + by(i)) for i in range(peers)]
        return lax.ppermute(array, "seq", [(i, j) for i, j in pairs if 0 <= j < peers])

    near = lambda i: -GROUP if i % GROUP < GROUP // 2 else GROUP
    far = lambda i: -near(i)

    kv = split_columns(others, key, value)
    kv_group = [kv[0]] + [swap(kv[m], m) for m in range(1, GROUP)]
    kv_halo = [move(kv_group[m], near if m < 2 else far) for m in range(GROUP)]

    last = jnp.concatenate([query[rows - EDGE :], residual[rows - EDGE :]], axis=1)
    initial = jnp.concatenate([query[:EDGE], residual[:EDGE]], axis=1)
    before = move(last, lambda i: 1)
    after = move(initial, lambda i: -1)
    query_ext = jnp.concatenate([before[:, :width], query, after[:, :width]], axis=0)
    q_out = split_columns(others, query_ext)
    q_group = [q_out[0]] + [swap(q_out[m], m) for m in range(1, GROUP)]

    ends = jnp.cumsum(lengths).astype(jnp.int32)
    starts = ends - lengths
    n_utts = lengths.shape[0]
    q_rows = (rows + 2 * EDGE) // 2
    halves = jnp.arange(2, dtype=jnp.int32)
    block_first = base + others[:, None] * rows
    first_own = jnp.where(halves == 0, 0, q_rows - EDGE)
    last_own = jnp.where(halves == 0, q_rows - EDGE - 1, rows - 1)
    first_utt = utterance_of((block_first + first_own).reshape(-1), ends)
    last_utt = utterance_of((block_first + last_own).reshape(-1), ends)
    low = (jnp.maximum(starts[first_utt] - key_base, 0) // 16) * 16
    high = jnp.minimum(ends[last_utt] - key_base, keys)
    need = high - low
    most = -(-(q_rows + 2 * halo + 16) // LANES) * LANES
    widths = sorted({min(w, most) for w in (256, 512, 768, 1024, most)})
    taken = functools.reduce(
        lambda later, w: jnp.where(need <= w, w, later), widths[::-1], jnp.full_like(need, most)
    )
    low = jnp.minimum(low, keys - taken)
    meta = jnp.concatenate(
        [key_base[None], base + others * rows - EDGE, low, need]
    ).astype(jnp.int32)
    at_group = others + GROUP // 2
    at_halo = jnp.where(others < GROUP // 2, others + 3 * GROUP // 2, others - GROUP // 2)
    place = jnp.concatenate([at_group, at_halo]).astype(jnp.int32)
    pad = -n_utts % LANES
    lane_starts = jnp.pad(starts, (0, pad))[None, :]
    lane_ends = jnp.pad(ends, (0, pad))[None, :]
    ctx = attend(
        rows, q_rows, widths, meta, place, lane_starts, lane_ends, q_group, kv_group + kv_halo
    )
    ctx_group = [ctx[0]] + [swap(ctx[m], m) for m in range(1, GROUP)]

    block_rows = 32
    n_blocks = rows // block_rows
    block_tops = me * rows + jnp.arange(n_blocks, dtype=jnp.int32) * block_rows
    meta_out = jnp.concatenate(
        [
            (me * rows)[None],
            others,
            utterance_of(block_tops, ends),
            utterance_of(block_tops + block_rows - 1, ends),
        ]
    ).astype(jnp.int32)
    return finish(
        block_rows,
        meta_out,
        starts,
        ends,
        ctx_group,
        residual,
        before[:, width:],
        after[:, width:],
        depth_kernel,
        gain[None, :],
        shift[None, :],
    )


def solution(mesh):
    return jax.shard_map(
        local,
        mesh=mesh,
        in_specs=(
            P(("dp", "seq"), None),
            P(("dp", "seq"), None),
            P(("dp", "seq"), None),
            P(("dp", "seq"), None),
            P("dp"),
            P(),
            P(),
            P(),
        ),
        out_specs=P(("dp", "seq"), None),
        check_vma=False,
    )
```

```python
import functools

import jax
import jax.numpy as jnp
from jax import lax
from jax.experimental import pallas as pl
from jax.experimental.pallas import tpu as pltpu
from jax.sharding import PartitionSpec as P

HD = 64
LANES = 128
GROUP = 4
EDGE = 16
SAME = 2048.0
CALLS = ((3, 1), (2, 0))
TAILED = (1, GROUP - 1)
VMEM_LIMIT = 56 << 20

ANY = pl.BlockSpec(memory_space=pl.ANY)
VMEM = pl.BlockSpec(memory_space=pltpu.VMEM)
SMEM = pl.BlockSpec(memory_space=pltpu.SMEM)


def utterance_of(positions, ends):
    return jnp.sum((ends[None, :] <= positions[:, None]).astype(jnp.int32), axis=1)


def split_kernel(cols, which, query, key, value, residual, *refs):
    kv_outs, q_outs = refs[:GROUP], refs[GROUP : 2 * GROUP]
    q_buf, kv_buf, edges, tail, in_sem, out_sem = refs[2 * GROUP :]
    rows = q_buf.shape[0]
    half = rows // 2
    loads = []
    for i, (src, dst) in enumerate(
        ((key, kv_buf.at[0]), (value, kv_buf.at[1]), (query, q_buf))
    ):
        for part in range(2):
            at = pl.ds(part * half, half)
            loads.append(
                pltpu.make_async_copy(src.at[at, :], dst.at[at, :], in_sem.at[2 * i + part])
            )
    for load in loads:
        load.start()
    tails = [None] * GROUP
    for m in TAILED:
        if m == 1:
            up = which[m] > which[0]
        else:
            up = (which[0] == 1) | (which[0] == GROUP - 1)
        at = pl.multiple_of(jnp.where(up, rows - EDGE, 0), EDGE)
        tails[m] = pltpu.make_async_copy(residual.at[pl.ds(at, EDGE), :], tail.at[m], in_sem.at[6 + m])
        tails[m].start()
    stores = []

    def store(src, dst):
        copy = pltpu.make_async_copy(src, dst, out_sem.at[len(stores)])
        copy.start()
        stores.append(copy)

    firsts = [pl.multiple_of(which[m] * cols, LANES) for m in range(GROUP)]
    for i in range(2):
        loads[2 * i].wait()
        loads[2 * i + 1].wait()
        for m in range(GROUP):
            store(
                kv_buf.at[i, :, pl.ds(firsts[m], cols)],
                kv_outs[m].at[pl.ds(0, rows), pl.ds(i * cols, cols)],
            )
    loads[4].wait()
    loads[5].wait()
    for m in range(GROUP):
        store(q_buf.at[:, pl.ds(firsts[m], cols)], q_outs[m])
        edges[m, :, :cols] = q_buf[:EDGE, pl.ds(firsts[m], cols)]
        edges[m, :, cols:] = q_buf[rows - EDGE :, pl.ds(firsts[m], cols)]
    for m in TAILED:
        tails[m].wait()
    for m in range(GROUP):
        store(edges.at[m], kv_outs[m].at[pl.ds(rows, EDGE), :])
        for part in range(2 if m in TAILED else 0):
            store(
                tail.at[m, :, pl.ds(part * 2 * cols, 2 * cols)],
                kv_outs[m].at[pl.ds(rows + (1 + part) * EDGE, EDGE), :],
            )
    for copy in stores:
        copy.wait()


def split_columns(which, query, key, value, residual):
    rows, width = query.shape
    cols = width // GROUP
    kind = query.dtype
    dma = pltpu.SemaphoreType.DMA
    got = pl.pallas_call(
        functools.partial(split_kernel, cols),
        out_shape=[
            jax.ShapeDtypeStruct((rows + (3 if m in TAILED else 1) * EDGE, 2 * cols), kind)
            for m in range(GROUP)
        ]
        + [jax.ShapeDtypeStruct((rows, cols), kind)] * GROUP,
        in_specs=[SMEM] + [ANY] * 4,
        out_specs=[ANY] * (2 * GROUP),
        scratch_shapes=[
            pltpu.VMEM((rows, width), kind),
            pltpu.VMEM((2, rows, width), kind),
            pltpu.VMEM((GROUP, EDGE, 2 * cols), kind),
            pltpu.VMEM((GROUP, EDGE, width), kind),
            dma((6 + GROUP,)),
            dma((4 * GROUP + 2 * len(TAILED),)),
        ],
        compiler_params=pltpu.CompilerParams(vmem_limit_bytes=VMEM_LIMIT),
        name="split_columns",
    )(which, query, key, value, residual)
    return got[:GROUP], got[GROUP:]


def attend_kernel(rows, q_rows, widths, n_out, meta, place, starts, ends, *refs):
    q_in, kv_in = refs[:GROUP], refs[GROUP : 3 * GROUP]
    outs = refs[3 * GROUP : 3 * GROUP + n_out]
    q_buf, kv_buf, oh_buf, edges, ctx_buf, q_sem, kv_sem, edge_sem, out_sem = refs[
        3 * GROUP + n_out :
    ]
    cols = q_buf.shape[1]
    blocks = ctx_buf.shape[1] // q_rows
    copies = []
    for i, src in enumerate(kv_in):
        at = pl.multiple_of(place[i] * rows, 16)
        src_rows = src.at[pl.ds(0, rows), :]
        copies.append(pltpu.make_async_copy(src_rows, kv_buf.at[pl.ds(at, rows), :], kv_sem.at[i]))
    for m, src in enumerate(q_in):
        at = pl.multiple_of((place[m] - GROUP // 2) * rows + EDGE, 16)
        copies.append(pltpu.make_async_copy(src, q_buf.at[pl.ds(at, rows), :], q_sem.at[m]))
    for m, src in enumerate(kv_in[GROUP:]):
        src_rows = src.at[pl.ds(rows, EDGE), :]
        copies.append(pltpu.make_async_copy(src_rows, edges.at[place[GROUP + m]], edge_sem.at[m]))
    for copy in copies:
        copy.start()

    def one_hot(first, n, value):
        frame = first + lax.broadcasted_iota(jnp.int32, (n, starts.shape[1]), 0)
        inside = (frame >= starts[...]) & (frame < ends[...])
        return jnp.where(inside, jnp.float32(value), jnp.float32(0.0)).astype(jnp.bfloat16)

    step = rows // 2

    @pl.loop(0, kv_buf.shape[0] // step)
    def _(i):
        at = pl.multiple_of(i * step, 16)
        oh_buf[pl.ds(at, step), :] = one_hot(meta[0] + at, step, 1.0)

    for copy in copies:
        copy.wait()
    q_buf[:EDGE, :] = edges[GROUP // 2 - 1, :, cols:]
    q_buf[EDGE + GROUP * rows :, :] = edges[GROUP + GROUP // 2, :, :cols]

    lane = lax.broadcasted_iota(jnp.int32, (1, LANES), 1)
    scale = HD**-0.5
    halves = [
        jnp.where(lane // HD == h, jnp.float32(scale), jnp.float32(0.0)).astype(jnp.bfloat16)
        for h in range(2)
    ]

    def block(m, b, low, first, width):
        at = pl.multiple_of(b * q_rows, 16)
        oh_q = one_hot(meta[1] + first, q_rows, SAME)
        oh_k = oh_buf[pl.ds(low, width), :]
        ones = jnp.ones((width, LANES), jnp.bfloat16)
        for pair in range(cols // LANES):
            at_cols = slice(pair * LANES, (pair + 1) * LANES)
            v_cols = slice(cols + pair * LANES, cols + (pair + 1) * LANES)
            q = q_buf[pl.ds(first, q_rows), at_cols]
            k = jnp.concatenate([kv_buf[pl.ds(low, width), at_cols], oh_k], axis=1)
            v = jnp.concatenate([kv_buf[pl.ds(low, width), v_cols], ones], axis=1)
            got = []
            for h in range(2):
                q_h = jnp.concatenate([q * halves[h], oh_q], axis=1)
                s = lax.dot_general(
                    q_h, k, (((1,), (1,)), ((), ())), preferred_element_type=jnp.float32
                )
                p = jnp.exp(s - jnp.max(s, axis=1, keepdims=True)).astype(jnp.bfloat16)
                o = jnp.dot(p, v, preferred_element_type=jnp.float32)
                got.append(o[:, :LANES] / o[:, LANES:])
            ctx = jnp.where(lane < HD, got[0], got[1]).astype(jnp.bfloat16)
            ctx_buf[m, pl.ds(at, q_rows), at_cols] = ctx

    @pl.loop(0, n_out * blocks)
    def _(t):
        m, b = t // blocks, t % blocks
        first = pl.multiple_of(meta[2 + t], 16)
        low = pl.multiple_of(meta[2 + n_out * blocks + t], 16)
        need = meta[2 + 2 * n_out * blocks + t]
        below = 0
        for width in widths:

            @pl.when((need > below) & (need <= width))
            def _(width=width):
                block(m, b, low, first, width)

            below = width

    copies = [
        pltpu.make_async_copy(ctx_buf.at[m], outs[m], out_sem.at[m]) for m in range(n_out)
    ]
    for copy in copies:
        copy.start()
    for copy in copies:
        copy.wait()


def attend(rows, q_rows, widths, meta, place, starts, ends, q_parts, kv_parts, n_out):
    cols = q_parts[0].shape[1]
    keys = 2 * GROUP * rows
    ext = rows + 2 * EDGE
    shape = jax.ShapeDtypeStruct((ext, cols), jnp.bfloat16)
    dma = pltpu.SemaphoreType.DMA
    return pl.pallas_call(
        functools.partial(attend_kernel, rows, q_rows, widths, n_out),
        out_shape=[shape] * n_out,
        in_specs=[SMEM, SMEM, VMEM, VMEM] + [ANY] * (3 * GROUP),
        out_specs=[ANY] * n_out,
        scratch_shapes=[
            pltpu.VMEM((GROUP * rows + 2 * EDGE, cols), jnp.bfloat16),
            pltpu.VMEM((keys, 2 * cols), jnp.bfloat16),
            pltpu.VMEM((keys, starts.shape[1]), jnp.bfloat16),
            pltpu.VMEM((2 * GROUP, EDGE, 2 * cols), jnp.bfloat16),
            pltpu.VMEM((n_out, ext, cols), jnp.bfloat16),
            dma((GROUP,)),
            dma((2 * GROUP,)),
            dma((GROUP,)),
            dma((n_out,)),
        ],
        compiler_params=pltpu.CompilerParams(vmem_limit_bytes=VMEM_LIMIT),
        cost_estimate=pl.CostEstimate(
            flops=n_out * 4 * ext * cols * keys, bytes_accessed=8 * keys * cols, transcendentals=0
        ),
        name="attend",
    )(meta, place, starts, ends, *q_parts, *kv_parts)


def finish_kernel(block_rows, taps, meta, starts, ends, *refs):
    ctx_in = refs[:GROUP]
    res, res_before, res_after, kernel, gain, shift, out = refs[GROUP : GROUP + 7]
    mixed, window, conv = refs[GROUP + 7 :]
    rows, width = res.shape
    tiles = width // LANES
    per = tiles // GROUP
    half = taps // 2
    n_blocks = rows // block_rows
    for m in range(GROUP):
        for t in range(per):
            cols = slice(t * LANES, (t + 1) * LANES)
            mixed[meta[1 + m] * per + t] = ctx_in[m][:, cols].astype(jnp.float32)
    for t in range(tiles):
        cols = slice(t * LANES, (t + 1) * LANES)
        for first, part in ((0, res_before), (EDGE, res), (EDGE + rows, res_after)):
            at = slice(first, first + part.shape[0])
            total = part[:, cols].astype(jnp.float32) + mixed[t, at, :]
            mixed[t, at, :] = total.astype(jnp.bfloat16).astype(jnp.float32)

    span = block_rows + 2 * EDGE

    @pl.loop(0, n_blocks)
    def _(b):
        top = pl.multiple_of(b * block_rows, 8)
        first_frame = meta[0] + top
        around = first_frame - EDGE + lax.broadcasted_iota(jnp.int32, (span, LANES), 0)
        frame = first_frame + lax.broadcasted_iota(jnp.int32, (block_rows, LANES), 0)

        @pl.loop(meta[1 + GROUP + b], meta[1 + GROUP + n_blocks + b] + 1)
        def _(u):
            low, high = starts[u], ends[u]
            kept = (around >= low) & (around < high)
            mine = (frame >= low) & (frame < high)
            for t in range(tiles):
                window[t] = jnp.where(kept, mixed[t, pl.ds(top, span), :], jnp.float32(0.0))
            for t in range(tiles):
                cols = slice(t * LANES, (t + 1) * LANES)
                total = jnp.zeros((block_rows, LANES), jnp.float32)
                for tap in range(taps):
                    at = tap + EDGE - half
                    total = total + window[t, at : at + block_rows, :] * kernel[tap : tap + 1, cols]
                conv[t] = jnp.where(mine, total, conv[t])

        values = [conv[t] for t in range(tiles)]
        mean = jnp.sum(sum(values), axis=1, keepdims=True) / width
        centred = [x - mean for x in values]
        var = jnp.sum(sum([x * x for x in centred]), axis=1, keepdims=True) / width
        inverse = 1.0 / jnp.sqrt(var + 1e-05)
        for t in range(tiles):
            cols = slice(t * LANES, (t + 1) * LANES)
            normed = centred[t] * inverse * gain[:, cols] + shift[:, cols]
            gated = normed * jax.nn.sigmoid(normed)
            own = mixed[t, pl.ds(pl.multiple_of(top + EDGE, 8), block_rows), :]
            out[pl.ds(pl.multiple_of(top, 16), block_rows), cols] = (own + gated).astype(
                jnp.bfloat16
            )


def finish(block_rows, meta, starts, ends, ctx_parts, res, before, after, kernel, gain, shift):
    rows, width = res.shape
    tiles = width // LANES
    return pl.pallas_call(
        functools.partial(finish_kernel, block_rows, kernel.shape[0]),
        out_shape=jax.ShapeDtypeStruct((rows, width), jnp.bfloat16),
        in_specs=[SMEM, SMEM, SMEM] + [VMEM] * (GROUP + 6),
        out_specs=VMEM,
        scratch_shapes=[
            pltpu.VMEM((tiles, rows + 2 * EDGE, LANES), jnp.float32),
            pltpu.VMEM((tiles, block_rows + 2 * EDGE, LANES), jnp.float32),
            pltpu.VMEM((tiles, block_rows, LANES), jnp.float32),
        ],
        compiler_params=pltpu.CompilerParams(vmem_limit_bytes=VMEM_LIMIT),
        name="finish",
    )(meta, starts, ends, *ctx_parts, res, before, after, kernel, gain, shift)


def local(query, key, value, residual, lengths, depth_kernel, gain, shift):
    rows, width = query.shape
    peers = lax.axis_size("seq")
    frames = rows * peers
    me = lax.axis_index("seq")
    member = me % GROUP
    others = jnp.arange(GROUP, dtype=jnp.int32) ^ member
    halo = 2 * rows
    base = (me - member) * rows
    key_base = base - halo
    keys = GROUP * rows + 2 * halo

    def swap(array, m):
        return lax.ppermute(array, "seq", [(i, i ^ m) for i in range(peers)])

    def move(array, by):
        pairs = [(i, i + by(i)) for i in range(peers)]
        return lax.ppermute(array, "seq", [(i, j) for i, j in pairs if 0 <= j < peers])

    near = lambda i: -GROUP if i % GROUP < GROUP // 2 else GROUP
    far = lambda i: -near(i)

    kv, q_out = split_columns(others, query, key, value, residual)
    kv_group = [kv[0]] + [swap(kv[m], m) for m in range(1, GROUP)]
    kv_halo = [move(kv_group[m], near if m < 2 else far) for m in range(GROUP)]
    q_group = [q_out[0]]
    for m in range(1, GROUP):
        part, kv_group[m] = lax.optimization_barrier((q_out[m], kv_group[m]))
        q_group.append(swap(part, m))

    ends = jnp.cumsum(lengths).astype(jnp.int32)
    starts = ends - lengths
    n_utts = lengths.shape[0]
    q_rows = (rows + 2 * EDGE) // 2
    halves = jnp.arange(2, dtype=jnp.int32)
    most = -(-(q_rows + 2 * halo + 16) // LANES) * LANES
    widths = sorted({min(w, most) for w in (256, 512, 768, 1024, most)})
    at_group = others + GROUP // 2
    at_halo = jnp.where(others < GROUP // 2, others + 3 * GROUP // 2, others - GROUP // 2)
    place = jnp.concatenate([at_group, at_halo]).astype(jnp.int32)
    pad = -n_utts % LANES
    lane_starts = jnp.pad(starts, (0, pad))[None, :]
    lane_ends = jnp.pad(ends, (0, pad))[None, :]
    first_own = jnp.where(halves == 0, 0, q_rows - EDGE)
    last_own = jnp.where(halves == 0, q_rows - EDGE - 1, rows - 1)
    first_utt = utterance_of((base + others[:, None] * rows + first_own).reshape(-1), ends)
    last_utt = utterance_of((base + others[:, None] * rows + last_own).reshape(-1), ends)
    low = (jnp.maximum(starts[first_utt] - key_base, 0) // 16) * 16
    need = jnp.minimum(ends[last_utt] - key_base, keys) - low
    taken = functools.reduce(
        lambda later, w: jnp.where(need <= w, w, later), widths[::-1], jnp.full_like(need, most)
    )
    low = jnp.minimum(low, keys - taken)
    first = (others[:, None] * rows + halves * q_rows).reshape(-1)
    ctx_group = [None] * GROUP
    for ms in CALLS:
        t = [2 * m + h for m in ms for h in range(2)]
        pick = lambda x: jnp.stack([x[i] for i in t])
        meta = jnp.concatenate(
            [key_base[None], (base - EDGE)[None], pick(first), pick(low), pick(need)]
        ).astype(jnp.int32)
        ctx = attend(
            rows,
            q_rows,
            widths,
            meta,
            place,
            lane_starts,
            lane_ends,
            q_group,
            kv_group + kv_halo,
            len(ms),
        )
        for m, part in zip(ms, ctx):
            ctx_group[m] = swap(part, m) if m else part

    def tail_of(part):
        return jnp.concatenate([part[rows + EDGE : rows + 2 * EDGE], part[rows + 2 * EDGE :]], axis=1)

    near_tail, diagonal, beyond = tail_of(kv_group[1]), tail_of(kv_group[-1]), tail_of(kv_halo[-1])
    other_tail = jnp.where((member == 0) | (member == GROUP - 1), beyond, diagonal)
    odd = member % 2 == 1
    before = jnp.where(odd, near_tail, other_tail)
    after = jnp.where(odd, other_tail, near_tail)

    block_rows = 32
    n_blocks = rows // block_rows
    block_tops = me * rows + jnp.arange(n_blocks, dtype=jnp.int32) * block_rows
    meta_out = jnp.concatenate(
        [
            (me * rows)[None],
            others,
            utterance_of(block_tops, ends),
            utterance_of(block_tops + block_rows - 1, ends),
        ]
    ).astype(jnp.int32)
    return finish(
        block_rows,
        meta_out,
        starts,
        ends,
        ctx_group,
        residual,
        before,
        after,
        depth_kernel,
        gain[None, :],
        shift[None, :],
    )


def solution(mesh):
    return jax.shard_map(
        local,
        mesh=mesh,
        in_specs=(
            P(("dp", "seq"), None),
            P(("dp", "seq"), None),
            P(("dp", "seq"), None),
            P(("dp", "seq"), None),
            P("dp"),
            P(),
            P(),
            P(),
        ),
        out_specs=P(("dp", "seq"), None),
        check_vma=False,
    )
```

```python
import functools

import jax
import jax.numpy as jnp
from jax import lax
from jax.experimental import pallas as pl
from jax.experimental.pallas import tpu as pltpu
from jax.sharding import PartitionSpec as P

HD = 64
LANES = 128
GROUP = 4
EDGE = 16
SAME = 2048.0
TAILED = (1, GROUP - 1)
WITH_Q = (2, 3)
KV_BLOCKS = GROUP + 2
WIDTHS = (256, 512, 768, 1024)
SPLIT_VMEM = 56 << 20
ATTEND_VMEM = 24 << 20
FINISH_VMEM = 24 << 20

ANY = pl.BlockSpec(memory_space=pl.ANY)
VMEM = pl.BlockSpec(memory_space=pltpu.VMEM)
SMEM = pl.BlockSpec(memory_space=pltpu.SMEM)


def utterance_of(positions, ends):
    return jnp.sum((ends[None, :] <= positions[:, None]).astype(jnp.int32), axis=1)


def tail_rows(m):
    return 2 * EDGE if m in TAILED else 0


def split_kernel(cols, which, query, key, value, residual, *refs):
    kv_outs, q_outs = refs[:GROUP], refs[GROUP : 2 * GROUP - len(WITH_Q)]
    q_buf, kv_buf, edges, tail, in_sem, out_sem = refs[2 * GROUP - len(WITH_Q) :]
    rows = q_buf.shape[0]
    half = rows // 2
    loads = []
    for i, (src, dst) in enumerate(((key, kv_buf.at[0]), (value, kv_buf.at[1]), (query, q_buf))):
        for part in range(2):
            at = pl.ds(part * half, half)
            sem = in_sem.at[2 * i + part]
            loads.append(pltpu.make_async_copy(src.at[at, :], dst.at[at, :], sem))
    for load in loads:
        load.start()
    tails = [None] * GROUP
    for m in TAILED:
        if m == 1:
            up = which[m] > which[0]
        else:
            up = (which[0] == 1) | (which[0] == GROUP - 1)
        at = pl.multiple_of(jnp.where(up, rows - EDGE, 0), EDGE)
        src = residual.at[pl.ds(at, EDGE), :]
        tails[m] = pltpu.make_async_copy(src, tail.at[m], in_sem.at[6 + m])
        tails[m].start()
    stores = []

    def store(src, dst):
        copy = pltpu.make_async_copy(src, dst, out_sem.at[len(stores)])
        copy.start()
        stores.append(copy)

    mine = [pl.ds(pl.multiple_of(which[m] * cols, LANES), cols) for m in range(GROUP)]
    for i in range(2):
        loads[2 * i].wait()
        loads[2 * i + 1].wait()
        for m in range(GROUP):
            store(kv_buf.at[i, :, mine[m]], kv_outs[m].at[pl.ds(0, rows), pl.ds(i * cols, cols)])
    loads[4].wait()
    loads[5].wait()
    q_alone = [m for m in range(GROUP) if m not in WITH_Q]
    for m in range(GROUP):
        edges[m, :, :cols] = q_buf[:EDGE, mine[m]]
        edges[m, :, cols:] = q_buf[rows - EDGE :, mine[m]]
        if m in WITH_Q:
            at = pl.ds(rows + EDGE + tail_rows(m), half)
            for part in range(2):
                src = q_buf.at[pl.ds(part * half, half), mine[m]]
                store(src, kv_outs[m].at[at, pl.ds(part * cols, cols)])
        else:
            store(q_buf.at[:, mine[m]], q_outs[q_alone.index(m)])
    for m in TAILED:
        tails[m].wait()
        for part in range(2):
            at = pl.ds(rows + (1 + part) * EDGE, EDGE)
            store(tail.at[m, :, pl.ds(part * 2 * cols, 2 * cols)], kv_outs[m].at[at, :])
    for m in range(GROUP):
        store(edges.at[m], kv_outs[m].at[pl.ds(rows, EDGE), :])
    for copy in stores:
        copy.wait()


def split_columns(which, query, key, value, residual):
    rows, width = query.shape
    cols = width // GROUP
    kind = query.dtype
    dma = pltpu.SemaphoreType.DMA
    sizes = [
        rows + EDGE + tail_rows(m) + (rows // 2 if m in WITH_Q else 0) for m in range(GROUP)
    ]
    n_alone = GROUP - len(WITH_Q)
    got = pl.pallas_call(
        functools.partial(split_kernel, cols),
        out_shape=[jax.ShapeDtypeStruct((size, 2 * cols), kind) for size in sizes]
        + [jax.ShapeDtypeStruct((rows, cols), kind)] * n_alone,
        in_specs=[SMEM] + [ANY] * 4,
        out_specs=[ANY] * (GROUP + n_alone),
        scratch_shapes=[
            pltpu.VMEM((rows, width), kind),
            pltpu.VMEM((2, rows, width), kind),
            pltpu.VMEM((GROUP, EDGE, 2 * cols), kind),
            pltpu.VMEM((GROUP, EDGE, width), kind),
            dma((6 + GROUP,)),
            dma((4 * GROUP + 2 * len(TAILED) + len(WITH_Q),)),
        ],
        compiler_params=pltpu.CompilerParams(vmem_limit_bytes=SPLIT_VMEM),
        name="split_columns",
    )(which, query, key, value, residual)
    return got[:GROUP], got[GROUP:]


def attend_kernel(rows, q_rows, widths, q_at, meta, place, starts, ends, *refs):
    kv_in, q_in, outs = refs[:KV_BLOCKS], refs[KV_BLOCKS : KV_BLOCKS + 2], refs[KV_BLOCKS + 2 : KV_BLOCKS + 4]
    q_buf, kv_buf, oh_buf, edges, ctx_buf, q_sem, kv_sem, edge_sem, out_sem = refs[KV_BLOCKS + 4 :]
    cols = q_buf.shape[1]
    half = rows // 2
    blocks = ctx_buf.shape[1] // q_rows
    copies = []
    for i, src in enumerate(kv_in):
        at = pl.multiple_of(place[i] * rows, 16)
        src_rows = src.at[pl.ds(0, rows), :]
        copies.append(pltpu.make_async_copy(src_rows, kv_buf.at[pl.ds(at, rows), :], kv_sem.at[i]))
        src_rows = src.at[pl.ds(rows, EDGE), :]
        copies.append(pltpu.make_async_copy(src_rows, edges.at[place[i]], edge_sem.at[i]))
    for i, src in enumerate(q_in):
        at = pl.multiple_of(place[KV_BLOCKS + i] * rows + EDGE, 16)
        if q_at[i] is None:
            dst = q_buf.at[pl.ds(at, rows), :]
            copies.append(pltpu.make_async_copy(src, dst, q_sem.at[2 * i]))
        else:
            for part in range(2):
                part_of = src.at[pl.ds(q_at[i], half), pl.ds(part * cols, cols)]
                dst = q_buf.at[pl.ds(at + part * half, half), :]
                copies.append(pltpu.make_async_copy(part_of, dst, q_sem.at[2 * i + part]))
    for copy in copies:
        copy.start()

    def one_hot(first, n, value):
        frame = first + lax.broadcasted_iota(jnp.int32, (n, starts.shape[1]), 0)
        inside = (frame >= starts[...]) & (frame < ends[...])
        return jnp.where(inside, jnp.float32(value), jnp.float32(0.0)).astype(jnp.bfloat16)

    @pl.loop(0, kv_buf.shape[0] // half)
    def _(i):
        at = pl.multiple_of(i * half, 16)
        oh_buf[pl.ds(at, half), :] = one_hot(meta[0] + at, half, 1.0)

    for copy in copies:
        copy.wait()
    q_buf[:EDGE, :] = edges[1, :, cols:]
    q_buf[EDGE + 2 * rows :, :] = edges[KV_BLOCKS - 2, :, :cols]

    lane = lax.broadcasted_iota(jnp.int32, (1, LANES), 1)
    scale = HD**-0.5
    halves = [
        jnp.where(lane // HD == h, jnp.float32(scale), jnp.float32(0.0)).astype(jnp.bfloat16)
        for h in range(2)
    ]

    def block(m, b, low, first, width):
        at = pl.multiple_of(b * q_rows, 16)
        oh_q = one_hot(meta[1] + first, q_rows, SAME)
        oh_k = oh_buf[pl.ds(low, width), :]
        oh_both = jnp.concatenate([oh_q, oh_q], axis=0)
        for pair in range(cols // LANES):
            at_cols = slice(pair * LANES, (pair + 1) * LANES)
            v_cols = slice(cols + pair * LANES, cols + (pair + 1) * LANES)
            q = q_buf[pl.ds(first, q_rows), at_cols]
            k = jnp.concatenate([kv_buf[pl.ds(low, width), at_cols], oh_k], axis=1)
            v = kv_buf[pl.ds(low, width), v_cols]
            q_both = jnp.concatenate([q * halves[0], q * halves[1]], axis=0)
            q_both = jnp.concatenate([q_both, oh_both], axis=1)
            s = lax.dot_general(
                q_both, k, (((1,), (1,)), ((), ())), preferred_element_type=jnp.float32
            )
            p = jnp.exp(s - jnp.max(s, axis=1, keepdims=True))
            denom = jnp.sum(p, axis=1, keepdims=True)
            o = jnp.dot(p.astype(jnp.bfloat16), v, preferred_element_type=jnp.float32) / denom
            ctx = jnp.where(lane < HD, o[:q_rows], o[q_rows:])
            ctx_buf[m, pl.ds(at, q_rows), at_cols] = ctx.astype(jnp.bfloat16)

    @pl.loop(0, 2 * blocks)
    def _(t):
        m, b = t // blocks, t % blocks
        first = pl.multiple_of(meta[2 + t], 16)
        low = pl.multiple_of(meta[2 + 2 * blocks + t], 16)
        need = meta[2 + 4 * blocks + t]
        below = 0
        for width in widths:

            @pl.when((need > below) & (need <= width))
            def _(width=width):
                block(m, b, low, first, width)

            below = width

    copies = [pltpu.make_async_copy(ctx_buf.at[m], outs[m], out_sem.at[m]) for m in range(2)]
    for copy in copies:
        copy.start()
    for copy in copies:
        copy.wait()


def attend(rows, cols, q_rows, widths, q_at, meta, place, starts, ends, kv_parts, q_parts):
    keys = KV_BLOCKS * rows
    ext = rows + 2 * EDGE
    shape = jax.ShapeDtypeStruct((ext, cols), jnp.bfloat16)
    dma = pltpu.SemaphoreType.DMA
    return pl.pallas_call(
        functools.partial(attend_kernel, rows, q_rows, widths, q_at),
        out_shape=[shape] * 2,
        in_specs=[SMEM, SMEM, VMEM, VMEM] + [ANY] * (KV_BLOCKS + 2),
        out_specs=[ANY] * 2,
        scratch_shapes=[
            pltpu.VMEM((2 * rows + 2 * EDGE, cols), jnp.bfloat16),
            pltpu.VMEM((keys, 2 * cols), jnp.bfloat16),
            pltpu.VMEM((keys, starts.shape[1]), jnp.bfloat16),
            pltpu.VMEM((KV_BLOCKS, EDGE, 2 * cols), jnp.bfloat16),
            pltpu.VMEM((2, ext, cols), jnp.bfloat16),
            dma((4,)),
            dma((KV_BLOCKS,)),
            dma((KV_BLOCKS,)),
            dma((2,)),
        ],
        compiler_params=pltpu.CompilerParams(vmem_limit_bytes=ATTEND_VMEM),
        cost_estimate=pl.CostEstimate(
            flops=32 * ext * cols * keys, bytes_accessed=8 * keys * cols, transcendentals=0
        ),
        name="attend",
    )(meta, place, starts, ends, *kv_parts, *q_parts)


def finish_kernel(block_rows, taps, meta, starts, ends, *refs):
    ctx_in = refs[:GROUP]
    res, res_before, res_after, kernel, gain, shift, out = refs[GROUP : GROUP + 7]
    mixed, window, conv = refs[GROUP + 7 :]
    rows, width = res.shape
    tiles = width // LANES
    per = tiles // GROUP
    half = taps // 2
    n_blocks = rows // block_rows
    for m in range(GROUP):
        for t in range(per):
            cols = slice(t * LANES, (t + 1) * LANES)
            mixed[meta[1 + m] * per + t] = ctx_in[m][:, cols].astype(jnp.float32)
    for t in range(tiles):
        cols = slice(t * LANES, (t + 1) * LANES)
        for first, part in ((0, res_before), (EDGE, res), (EDGE + rows, res_after)):
            at = slice(first, first + part.shape[0])
            total = part[:, cols].astype(jnp.float32) + mixed[t, at, :]
            mixed[t, at, :] = total.astype(jnp.bfloat16).astype(jnp.float32)

    span = block_rows + 2 * EDGE

    @pl.loop(0, n_blocks)
    def _(b):
        top = pl.multiple_of(b * block_rows, 8)
        first_frame = meta[0] + top
        around = first_frame - EDGE + lax.broadcasted_iota(jnp.int32, (span, LANES), 0)
        frame = first_frame + lax.broadcasted_iota(jnp.int32, (block_rows, LANES), 0)

        @pl.loop(meta[1 + GROUP + b], meta[1 + GROUP + n_blocks + b] + 1)
        def _(u):
            low, high = starts[u], ends[u]
            kept = (around >= low) & (around < high)
            mine = (frame >= low) & (frame < high)
            for t in range(tiles):
                window[t] = jnp.where(kept, mixed[t, pl.ds(top, span), :], jnp.float32(0.0))
            for t in range(tiles):
                cols = slice(t * LANES, (t + 1) * LANES)
                total = jnp.zeros((block_rows, LANES), jnp.float32)
                for tap in range(taps):
                    at = tap + EDGE - half
                    total = total + window[t, at : at + block_rows, :] * kernel[tap : tap + 1, cols]
                conv[t] = jnp.where(mine, total, conv[t])

        values = [conv[t] for t in range(tiles)]
        mean = jnp.sum(sum(values), axis=1, keepdims=True) / width
        centred = [x - mean for x in values]
        var = jnp.sum(sum([x * x for x in centred]), axis=1, keepdims=True) / width
        inverse = 1.0 / jnp.sqrt(var + 1e-05)
        for t in range(tiles):
            cols = slice(t * LANES, (t + 1) * LANES)
            normed = centred[t] * inverse * gain[:, cols] + shift[:, cols]
            gated = normed * jax.nn.sigmoid(normed)
            own = mixed[t, pl.ds(pl.multiple_of(top + EDGE, 8), block_rows), :]
            out[pl.ds(pl.multiple_of(top, 16), block_rows), cols] = (own + gated).astype(
                jnp.bfloat16
            )


def finish(block_rows, meta, starts, ends, ctx_parts, res, before, after, kernel, gain, shift):
    rows, width = res.shape
    tiles = width // LANES
    return pl.pallas_call(
        functools.partial(finish_kernel, block_rows, kernel.shape[0]),
        out_shape=jax.ShapeDtypeStruct((rows, width), jnp.bfloat16),
        in_specs=[SMEM, SMEM, SMEM] + [VMEM] * (GROUP + 6),
        out_specs=VMEM,
        scratch_shapes=[
            pltpu.VMEM((tiles, rows + 2 * EDGE, LANES), jnp.float32),
            pltpu.VMEM((tiles, block_rows + 2 * EDGE, LANES), jnp.float32),
            pltpu.VMEM((tiles, block_rows, LANES), jnp.float32),
        ],
        compiler_params=pltpu.CompilerParams(vmem_limit_bytes=FINISH_VMEM),
        name="finish",
    )(meta, starts, ends, *ctx_parts, res, before, after, kernel, gain, shift)


def local(query, key, value, residual, lengths, depth_kernel, gain, shift):
    rows, width = query.shape
    peers = lax.axis_size("seq")
    frames = rows * peers
    me = lax.axis_index("seq")
    member = me % GROUP
    others = jnp.arange(GROUP, dtype=jnp.int32) ^ member
    halo = 2 * rows
    base = (me - member) * rows

    def swap(array, m):
        return lax.ppermute(array, "seq", [(i, i ^ m) for i in range(peers)])

    def move(array, by):
        pairs = [(i, i + by(i)) for i in range(peers)]
        return lax.ppermute(array, "seq", [(i, j) for i, j in pairs if 0 <= j < peers])

    near = lambda i: -GROUP if i % GROUP < GROUP // 2 else GROUP
    far = lambda i: -near(i)

    kv, q_alone = split_columns(others, query, key, value, residual)
    kv_group = [kv[0]] + [swap(kv[m], m) for m in range(1, GROUP)]
    q_near = [swap(q_alone[1], 1), q_alone[0]]
    bare = [part[: rows + EDGE + tail_rows(m)] for m, part in enumerate(kv_group)]
    kv_halo = [move(bare[m], near if m < 2 else far) for m in range(GROUP)]

    ends = jnp.cumsum(lengths).astype(jnp.int32)
    starts = ends - lengths
    n_utts = lengths.shape[0]
    keys = KV_BLOCKS * rows
    q_rows = (rows + 2 * EDGE) // 2
    halves = jnp.arange(2, dtype=jnp.int32)
    most = -(-(q_rows + 2 * halo + 16) // LANES) * LANES
    widths = sorted({min(w, most) for w in WIDTHS + (most,)})
    pad = -n_utts % LANES
    lane_starts = jnp.pad(starts, (0, pad))[None, :]
    lane_ends = jnp.pad(ends, (0, pad))[None, :]
    first_own = jnp.where(halves == 0, 0, q_rows - EDGE)
    last_own = jnp.where(halves == 0, q_rows - EDGE - 1, rows - 1)

    def attend_pair(ms, kv_parts, q_parts, q_at):
        at = others[ms[0]] // 2
        block_at = jnp.stack([others[m] for m in ms])
        key_base = base + (2 * at - 2) * rows
        first_utt = utterance_of((base + block_at[:, None] * rows + first_own).reshape(-1), ends)
        last_utt = utterance_of((base + block_at[:, None] * rows + last_own).reshape(-1), ends)
        low = (jnp.maximum(starts[first_utt] - key_base, 0) // 16) * 16
        need = jnp.minimum(ends[last_utt] - key_base, keys) - low
        taken = functools.reduce(
            lambda later, w: jnp.where(need <= w, w, later), widths[::-1], jnp.full_like(need, most)
        )
        low = jnp.minimum(low, keys - taken)
        first = ((block_at % 2)[:, None] * rows + halves * q_rows).reshape(-1)
        q_base = base + 2 * at * rows - EDGE
        meta = jnp.concatenate([key_base[None], q_base[None], first, low, need]).astype(jnp.int32)
        halo_at = jnp.stack([others[m] for m in (0, 1)] if ms[0] > 1 else [others[m] for m in (2, 3)])
        place = jnp.concatenate(
            [others - 2 * at + 2, halo_at % 2 + 4 * at, block_at % 2]
        ).astype(jnp.int32)
        return attend(
            rows,
            width // GROUP,
            q_rows,
            widths,
            q_at,
            meta,
            place,
            lane_starts,
            lane_ends,
            kv_parts,
            q_parts,
        )

    q_at = tuple(rows + EDGE + tail_rows(m) for m in (3, 2))
    ctx_far = attend_pair((3, 2), kv_group + kv_halo[:2], [kv_group[3], kv_group[2]], q_at)
    ctx_3, ctx_2 = swap(ctx_far[0], 3), swap(ctx_far[1], 2)
    ctx_near = attend_pair((1, 0), kv_group + kv_halo[2:], q_near, (None, None))
    ctx_group = [ctx_near[1], swap(ctx_near[0], 1), ctx_2, ctx_3]

    def tail_of(part):
        return jnp.concatenate([part[rows + EDGE : rows + 2 * EDGE], part[rows + 2 * EDGE : rows + 3 * EDGE]], axis=1)

    near_tail, diagonal, beyond = tail_of(kv_group[1]), tail_of(kv_group[-1]), tail_of(kv_halo[-1])
    other_tail = jnp.where((member == 0) | (member == GROUP - 1), beyond, diagonal)
    odd = member % 2 == 1
    before = jnp.where(odd, near_tail, other_tail)
    after = jnp.where(odd, other_tail, near_tail)

    block_rows = 32
    n_blocks = rows // block_rows
    block_tops = me * rows + jnp.arange(n_blocks, dtype=jnp.int32) * block_rows
    meta_out = jnp.concatenate(
        [
            (me * rows)[None],
            others,
            utterance_of(block_tops, ends),
            utterance_of(block_tops + block_rows - 1, ends),
        ]
    ).astype(jnp.int32)
    return finish(
        block_rows,
        meta_out,
        starts,
        ends,
        ctx_group,
        residual,
        before,
        after,
        depth_kernel,
        gain[None, :],
        shift[None, :],
    )


def solution(mesh):
    return jax.shard_map(
        local,
        mesh=mesh,
        in_specs=(
            P(("dp", "seq"), None),
            P(("dp", "seq"), None),
            P(("dp", "seq"), None),
            P(("dp", "seq"), None),
            P("dp"),
            P(),
            P(),
            P(),
        ),
        out_specs=P(("dp", "seq"), None),
        check_vma=False,
    )
```

```python
import functools

import jax
import jax.numpy as jnp
from jax import lax
from jax.experimental import pallas as pl
from jax.experimental.pallas import tpu as pltpu
from jax.sharding import PartitionSpec as P

HD = 64
LANES = 128
GROUP = 4
EDGE = 16
SAME = 2048.0
TAILED = (1, GROUP - 1)
WITH_Q = (2, 3)
KV_BLOCKS = GROUP + 2
WIDTHS = (256, 512, 768, 1024)
BLOCK_ROWS = 32
SPLIT_VMEM = 56 << 20
ATTEND_VMEM = 24 << 20
FINISH_VMEM = 24 << 20

ANY = pl.BlockSpec(memory_space=pl.ANY)
VMEM = pl.BlockSpec(memory_space=pltpu.VMEM)
SMEM = pl.BlockSpec(memory_space=pltpu.SMEM)


def group_place(rows):
    me = lax.axis_index("seq")
    member = me % GROUP
    return member, (me - member) * rows, [lax.bitwise_xor(member, m) for m in range(GROUP)]


def tail_rows(m):
    return 2 * EDGE if m in TAILED else 0


def split_kernel(cols, query, key, value, residual, *refs):
    kv_outs, q_outs = refs[:GROUP], refs[GROUP : 2 * GROUP - len(WITH_Q)]
    q_buf, kv_buf, edges, tail, in_sem, out_sem = refs[2 * GROUP - len(WITH_Q) :]
    rows = q_buf.shape[0]
    half = rows // 2
    _, _, which = group_place(rows)
    loads = []
    for i, (src, dst) in enumerate(((key, kv_buf.at[0]), (value, kv_buf.at[1]), (query, q_buf))):
        for part in range(2):
            at = pl.ds(part * half, half)
            sem = in_sem.at[2 * i + part]
            loads.append(pltpu.make_async_copy(src.at[at, :], dst.at[at, :], sem))
    for load in loads:
        load.start()
    tails = [None] * GROUP
    for m in TAILED:
        if m == 1:
            up = which[m] > which[0]
        else:
            up = (which[0] == 1) | (which[0] == GROUP - 1)
        at = pl.multiple_of(jnp.where(up, rows - EDGE, 0), EDGE)
        src = residual.at[pl.ds(at, EDGE), :]
        tails[m] = pltpu.make_async_copy(src, tail.at[m], in_sem.at[6 + m])
        tails[m].start()
    stores = []

    def store(src, dst):
        copy = pltpu.make_async_copy(src, dst, out_sem.at[len(stores)])
        copy.start()
        stores.append(copy)

    mine = [pl.ds(pl.multiple_of(which[m] * cols, LANES), cols) for m in range(GROUP)]
    for i in range(2):
        loads[2 * i].wait()
        loads[2 * i + 1].wait()
        for m in range(GROUP):
            store(kv_buf.at[i, :, mine[m]], kv_outs[m].at[pl.ds(0, rows), pl.ds(i * cols, cols)])
    loads[4].wait()
    loads[5].wait()
    q_alone = [m for m in range(GROUP) if m not in WITH_Q]
    for m in range(GROUP):
        edges[m, :, :cols] = q_buf[:EDGE, mine[m]]
        edges[m, :, cols:] = q_buf[rows - EDGE :, mine[m]]
        if m in WITH_Q:
            at = pl.ds(rows + EDGE + tail_rows(m), half)
            for part in range(2):
                src = q_buf.at[pl.ds(part * half, half), mine[m]]
                store(src, kv_outs[m].at[at, pl.ds(part * cols, cols)])
        else:
            store(q_buf.at[:, mine[m]], q_outs[q_alone.index(m)])
    for m in TAILED:
        tails[m].wait()
        for part in range(2):
            at = pl.ds(rows + (1 + part) * EDGE, EDGE)
            store(tail.at[m, :, pl.ds(part * 2 * cols, 2 * cols)], kv_outs[m].at[at, :])
    for m in range(GROUP):
        store(edges.at[m], kv_outs[m].at[pl.ds(rows, EDGE), :])
    for copy in stores:
        copy.wait()


def split_columns(query, key, value, residual):
    rows, width = query.shape
    cols = width // GROUP
    kind = query.dtype
    dma = pltpu.SemaphoreType.DMA
    sizes = [
        rows + EDGE + tail_rows(m) + (rows // 2 if m in WITH_Q else 0) for m in range(GROUP)
    ]
    n_alone = GROUP - len(WITH_Q)
    got = pl.pallas_call(
        functools.partial(split_kernel, cols),
        out_shape=[jax.ShapeDtypeStruct((size, 2 * cols), kind) for size in sizes]
        + [jax.ShapeDtypeStruct((rows, cols), kind)] * n_alone,
        in_specs=[ANY] * 4,
        out_specs=[ANY] * (GROUP + n_alone),
        scratch_shapes=[
            pltpu.VMEM((rows, width), kind),
            pltpu.VMEM((2, rows, width), kind),
            pltpu.VMEM((GROUP, EDGE, 2 * cols), kind),
            pltpu.VMEM((GROUP, EDGE, width), kind),
            dma((6 + GROUP,)),
            dma((4 * GROUP + 2 * len(TAILED) + len(WITH_Q),)),
        ],
        compiler_params=pltpu.CompilerParams(vmem_limit_bytes=SPLIT_VMEM),
        name="split_columns",
    )(query, key, value, residual)
    return got[:GROUP], got[GROUP:]


def attend_kernel(rows, q_rows, widths, ms, q_at, lengths, *refs):
    kv_in, q_in, outs = refs[:KV_BLOCKS], refs[KV_BLOCKS : KV_BLOCKS + 2], refs[KV_BLOCKS + 2 : KV_BLOCKS + 4]
    q_buf, kv_buf, oh_buf, edges, ctx_buf, q_sem, kv_sem, edge_sem, out_sem, meta = refs[
        KV_BLOCKS + 4 :
    ]
    cols = q_buf.shape[1]
    half = rows // 2
    blocks = ctx_buf.shape[1] // q_rows
    _, base, which = group_place(rows)
    pair = which[ms[0]] // 2
    key_base = base + (2 * pair - 2) * rows
    place = [w - 2 * pair + 2 for w in which]
    place += [which[m] % 2 + 4 * pair for m in range(GROUP) if m not in ms]
    place += [which[m] % 2 for m in ms]
    copies = []
    for i, src in enumerate(kv_in):
        at = pl.multiple_of(place[i] * rows, 16)
        src_rows = src.at[pl.ds(0, rows), :]
        copies.append(pltpu.make_async_copy(src_rows, kv_buf.at[pl.ds(at, rows), :], kv_sem.at[i]))
        src_rows = src.at[pl.ds(rows, EDGE), :]
        copies.append(pltpu.make_async_copy(src_rows, edges.at[place[i]], edge_sem.at[i]))
    for i, src in enumerate(q_in):
        at = pl.multiple_of(place[KV_BLOCKS + i] * rows + EDGE, 16)
        if q_at[i] is None:
            dst = q_buf.at[pl.ds(at, rows), :]
            copies.append(pltpu.make_async_copy(src, dst, q_sem.at[2 * i]))
        else:
            for part in range(2):
                part_of = src.at[pl.ds(q_at[i], half), pl.ds(part * cols, cols)]
                dst = q_buf.at[pl.ds(at + part * half, half), :]
                copies.append(pltpu.make_async_copy(part_of, dst, q_sem.at[2 * i + part]))
    for copy in copies:
        copy.start()

    utt_lane = lax.broadcasted_iota(jnp.int32, (1, oh_buf.shape[1]), 1)
    spans = []
    for m in ms:
        own = base + which[m] * rows
        spans += [(own, own + q_rows - EDGE - 1), (own + q_rows - EDGE, own + rows - 1)]

    def visit(u, carry):
        end, low_of, high_of, starts, ends = carry
        start, end = end, end + lengths[u]
        low_of = [jnp.where((a >= start) & (a < end), start, x) for (a, _), x in zip(spans, low_of)]
        high_of = [jnp.where((b >= start) & (b < end), end, x) for (_, b), x in zip(spans, high_of)]
        here = utt_lane == u
        return end, low_of, high_of, jnp.where(here, start, starts), jnp.where(here, end, ends)

    zero, none = jnp.int32(0), jnp.zeros(utt_lane.shape, jnp.int32)
    _, low_of, high_of, starts, ends = lax.fori_loop(
        0, lengths.shape[0], visit, (zero, [zero] * len(spans), [zero] * len(spans), none, none)
    )
    keys = kv_buf.shape[0]
    for t in range(len(spans)):
        low = jnp.maximum(low_of[t] - key_base, 0) // 16 * 16
        need = jnp.minimum(high_of[t] - key_base, keys) - low
        taken = widths[-1]
        for width in widths[-2::-1]:
            taken = jnp.where(need <= width, width, taken)
        meta[0, t] = jnp.minimum(low, keys - taken)
        meta[1, t] = need
        meta[2, t] = which[ms[t // blocks]] % 2 * rows + t % blocks * q_rows

    def one_hot(first, n, value):
        frame = first + lax.broadcasted_iota(jnp.int32, (n, utt_lane.shape[1]), 0)
        inside = (frame >= starts) & (frame < ends)
        return jnp.where(inside, jnp.float32(value), jnp.float32(0.0)).astype(jnp.bfloat16)

    @pl.loop(0, kv_buf.shape[0] // half)
    def _(i):
        at = pl.multiple_of(i * half, 16)
        oh_buf[pl.ds(at, half), :] = one_hot(key_base + at, half, 1.0)

    for copy in copies:
        copy.wait()
    q_buf[:EDGE, :] = edges[1, :, cols:]
    q_buf[EDGE + 2 * rows :, :] = edges[KV_BLOCKS - 2, :, :cols]

    lane = lax.broadcasted_iota(jnp.int32, (1, LANES), 1)
    scale = HD**-0.5
    halves = [
        jnp.where(lane // HD == h, jnp.float32(scale), jnp.float32(0.0)).astype(jnp.bfloat16)
        for h in range(2)
    ]

    def block(m, b, low, first, width):
        at = pl.multiple_of(b * q_rows, 16)
        oh_q = one_hot(key_base + 2 * rows - EDGE + first, q_rows, SAME)
        oh_k = oh_buf[pl.ds(low, width), :]
        oh_both = jnp.concatenate([oh_q, oh_q], axis=0)
        for p_at in range(0, cols, LANES):
            at_cols = slice(p_at, p_at + LANES)
            v_cols = slice(cols + p_at, cols + p_at + LANES)
            q = q_buf[pl.ds(first, q_rows), at_cols]
            k = jnp.concatenate([kv_buf[pl.ds(low, width), at_cols], oh_k], axis=1)
            v = kv_buf[pl.ds(low, width), v_cols]
            q_both = jnp.concatenate([q * halves[0], q * halves[1]], axis=0)
            q_both = jnp.concatenate([q_both, oh_both], axis=1)
            s = lax.dot_general(
                q_both, k, (((1,), (1,)), ((), ())), preferred_element_type=jnp.float32
            )
            p = jnp.exp(s - jnp.max(s, axis=1, keepdims=True))
            denom = jnp.sum(p, axis=1, keepdims=True)
            o = jnp.dot(p.astype(jnp.bfloat16), v, preferred_element_type=jnp.float32) / denom
            ctx = jnp.where(lane < HD, o[:q_rows], o[q_rows:])
            ctx_buf[m, pl.ds(at, q_rows), at_cols] = ctx.astype(jnp.bfloat16)

    @pl.loop(0, 2 * blocks)
    def _(t):
        m, b = t // blocks, t % blocks
        low, need = pl.multiple_of(meta[0, t], 16), meta[1, t]
        first = pl.multiple_of(meta[2, t], 16)
        below = 0
        for width in widths:

            @pl.when((need > below) & (need <= width))
            def _(width=width):
                block(m, b, low, first, width)

            below = width

    copies = [pltpu.make_async_copy(ctx_buf.at[m], outs[m], out_sem.at[m]) for m in range(2)]
    for copy in copies:
        copy.start()
    for copy in copies:
        copy.wait()


def attend(rows, cols, ms, q_at, lengths, kv_parts, q_parts):
    keys = KV_BLOCKS * rows
    ext = rows + 2 * EDGE
    q_rows = ext // 2
    most = -(-(q_rows + 4 * rows + 16) // LANES) * LANES
    widths = sorted({min(w, most) for w in WIDTHS + (most,)})
    utts = -(-lengths.shape[0] // LANES) * LANES
    shape = jax.ShapeDtypeStruct((ext, cols), jnp.bfloat16)
    dma = pltpu.SemaphoreType.DMA
    return pl.pallas_call(
        functools.partial(attend_kernel, rows, q_rows, widths, ms, q_at),
        out_shape=[shape] * 2,
        in_specs=[SMEM] + [ANY] * (KV_BLOCKS + 2),
        out_specs=[ANY] * 2,
        scratch_shapes=[
            pltpu.VMEM((2 * rows + 2 * EDGE, cols), jnp.bfloat16),
            pltpu.VMEM((keys, 2 * cols), jnp.bfloat16),
            pltpu.VMEM((keys, utts), jnp.bfloat16),
            pltpu.VMEM((KV_BLOCKS, EDGE, 2 * cols), jnp.bfloat16),
            pltpu.VMEM((2, ext, cols), jnp.bfloat16),
            dma((4,)),
            dma((KV_BLOCKS,)),
            dma((KV_BLOCKS,)),
            dma((2,)),
            pltpu.SMEM((3, 4), jnp.int32),
        ],
        compiler_params=pltpu.CompilerParams(vmem_limit_bytes=ATTEND_VMEM),
        cost_estimate=pl.CostEstimate(
            flops=32 * ext * cols * keys, bytes_accessed=8 * keys * cols, transcendentals=0
        ),
        name="attend",
    )(lengths, *kv_parts, *q_parts)


def convolve(block_rows, ms, lengths, ctx_in, res, before, after, kernel, mixed_out, conv_out, scratch):
    mixed, window, starts, ends = scratch
    rows, width = res.shape
    _, base, which = group_place(rows)
    own = base + which[0] * rows
    per = width // LANES // GROUP
    taps = kernel.shape[0]
    half = taps // 2
    tiles = [
        (i, t, pl.ds(pl.multiple_of((which[m] * per + t) * LANES, LANES), LANES))
        for i, m in enumerate(ms)
        for t in range(per)
    ]

    def note(u, end):
        starts[u] = end
        ends[u] = end + lengths[u]
        return end + lengths[u]

    lax.fori_loop(0, lengths.shape[0], note, jnp.int32(0))
    for slot, (i, t, cols) in enumerate(tiles):
        ctx = ctx_in[i][:, t * LANES : (t + 1) * LANES].astype(jnp.float32)
        for first, part in ((0, before), (EDGE, res), (EDGE + rows, after)):
            at = slice(first, first + part.shape[0])
            total = (part[:, cols].astype(jnp.float32) + ctx[at]).astype(jnp.bfloat16)
            mixed[slot, at, :] = total.astype(jnp.float32)
            if part is res:
                mixed_out[slot] = total

    span = block_rows + 2 * EDGE

    def past(frame):
        return lambda u: ends[u] <= frame

    @pl.loop(0, rows // block_rows, init_carry=jnp.int32(0))
    def _(b, first_utt):
        top = pl.multiple_of(b * block_rows, 16)
        around = own + top - EDGE + lax.broadcasted_iota(jnp.int32, (span, LANES), 0)
        frame = own + top + lax.broadcasted_iota(jnp.int32, (block_rows, LANES), 0)
        first_utt = lax.while_loop(past(own + top), lambda u: u + 1, first_utt)
        last_utt = lax.while_loop(past(own + top + block_rows - 1), lambda u: u + 1, first_utt)

        @pl.loop(first_utt, last_utt + 1)
        def _(u):
            low, high = starts[u], ends[u]
            kept = (around >= low) & (around < high)
            mine = (frame >= low) & (frame < high)
            for slot in range(len(tiles)):
                window[slot] = jnp.where(kept, mixed[slot, pl.ds(top, span), :], jnp.float32(0.0))
            for slot, (_, _, cols) in enumerate(tiles):
                total = jnp.zeros((block_rows, LANES), jnp.float32)
                for tap in range(taps):
                    at = tap + EDGE - half
                    total = total + window[slot, at : at + block_rows, :] * kernel[tap : tap + 1, cols]
                at = pl.ds(top, block_rows)
                conv_out[slot, at, :] = jnp.where(mine, total, conv_out[slot, at, :])

        return last_utt


def convolve_kernel(block_rows, ms, lengths, *refs):
    ctx_in = refs[: len(ms)]
    res, before, after, kernel, mixed_out, conv_out = refs[len(ms) : len(ms) + 6]
    scratch = refs[len(ms) + 6 :]
    convolve(block_rows, ms, lengths, ctx_in, res, before, after, kernel, mixed_out, conv_out, scratch)


def finish_kernel(block_rows, ms, early, lengths, *refs):
    ctx_in = refs[: len(ms)]
    res, before, after, kernel, gain, shift, mixed_in, conv_in, out = refs[len(ms) : len(ms) + 9]
    mixed_own, conv_own = refs[len(ms) + 9 : len(ms) + 11]
    scratch = refs[len(ms) + 11 :]
    convolve(block_rows, ms, lengths, ctx_in, res, before, after, kernel, mixed_own, conv_own, scratch)
    rows, width = res.shape
    _, _, which = group_place(rows)
    per = width // LANES // GROUP
    sources = []
    for group, mixed, conv in ((early, mixed_in, conv_in), (ms, mixed_own, conv_own)):
        for i, m in enumerate(group):
            for t in range(per):
                cols = pl.ds(pl.multiple_of((which[m] * per + t) * LANES, LANES), LANES)
                sources.append((mixed, conv, i * per + t, cols))

    @pl.loop(0, rows // block_rows)
    def _(b):
        at = pl.ds(pl.multiple_of(b * block_rows, 16), block_rows)
        values = [conv[slot, at, :] for _, conv, slot, _ in sources]
        mean = jnp.sum(sum(values), axis=1, keepdims=True) / width
        centred = [x - mean for x in values]
        var = jnp.sum(sum([x * x for x in centred]), axis=1, keepdims=True) / width
        inverse = 1.0 / jnp.sqrt(var + 1e-05)
        for x, (mixed, _, slot, cols) in zip(centred, sources):
            normed = x * inverse * gain[:, cols] + shift[:, cols]
            gated = normed * jax.nn.sigmoid(normed)
            out[at, cols] = (mixed[slot, at, :].astype(jnp.float32) + gated).astype(jnp.bfloat16)


def conv_scratch(slots, rows, block_rows, utts):
    return [
        pltpu.VMEM((slots, rows + 2 * EDGE, LANES), jnp.float32),
        pltpu.VMEM((slots, block_rows + 2 * EDGE, LANES), jnp.float32),
        pltpu.SMEM((utts,), jnp.int32),
        pltpu.SMEM((utts,), jnp.int32),
    ]


def convolve_early(ms, lengths, ctx_parts, res, before, after, kernel):
    rows, width = res.shape
    slots = len(ms) * width // LANES // GROUP
    taps = kernel.shape[0]
    return pl.pallas_call(
        functools.partial(convolve_kernel, BLOCK_ROWS, ms),
        out_shape=[
            jax.ShapeDtypeStruct((slots, rows, LANES), jnp.bfloat16),
            jax.ShapeDtypeStruct((slots, rows, LANES), jnp.float32),
        ],
        in_specs=[SMEM] + [VMEM] * (len(ms) + 4),
        out_specs=[VMEM] * 2,
        scratch_shapes=conv_scratch(slots, rows, BLOCK_ROWS, lengths.shape[0]),
        compiler_params=pltpu.CompilerParams(vmem_limit_bytes=FINISH_VMEM),
        cost_estimate=pl.CostEstimate(
            flops=100 * taps * rows * slots * LANES, bytes_accessed=8 * rows * width, transcendentals=0
        ),
        name="convolve",
    )(lengths, *ctx_parts, res, before, after, kernel)


def finish(ms, early, lengths, ctx_parts, res, before, after, kernel, gain, shift, mixed, conv):
    rows, width = res.shape
    slots = len(ms) * width // LANES // GROUP
    return pl.pallas_call(
        functools.partial(finish_kernel, BLOCK_ROWS, ms, early),
        out_shape=jax.ShapeDtypeStruct((rows, width), jnp.bfloat16),
        in_specs=[SMEM] + [VMEM] * (len(ms) + 8),
        out_specs=VMEM,
        scratch_shapes=[
            pltpu.VMEM((slots, rows, LANES), jnp.bfloat16),
            pltpu.VMEM((slots, rows, LANES), jnp.float32),
        ]
        + conv_scratch(slots, rows, BLOCK_ROWS, lengths.shape[0]),
        compiler_params=pltpu.CompilerParams(vmem_limit_bytes=FINISH_VMEM),
        name="finish",
    )(lengths, *ctx_parts, res, before, after, kernel, gain, shift, mixed, conv)


def local(query, key, value, residual, lengths, depth_kernel, gain, shift):
    rows, width = query.shape
    cols = width // GROUP
    peers = lax.axis_size("seq")

    def swap(array, m):
        return lax.ppermute(array, "seq", [(i, i ^ m) for i in range(peers)])

    def move(array, by):
        pairs = [(i, i + by(i)) for i in range(peers)]
        return lax.ppermute(array, "seq", [(i, j) for i, j in pairs if 0 <= j < peers])

    near = lambda i: -GROUP if i % GROUP < GROUP // 2 else GROUP
    far = lambda i: -near(i)

    kv, q_alone = split_columns(query, key, value, residual)
    kv_group = [kv[0]] + [swap(kv[m], m) for m in range(1, GROUP)]
    q_near = [swap(q_alone[1], 1), q_alone[0]]
    bare = [part[: rows + EDGE + tail_rows(m)] for m, part in enumerate(kv_group)]
    kv_halo = [move(bare[m], near if m < 2 else far) for m in range(GROUP)]

    q_at = tuple(rows + EDGE + tail_rows(m) for m in (3, 2))
    far_q = [kv_group[3], kv_group[2]]
    ctx_far = attend(rows, cols, (3, 2), q_at, lengths, kv_group + kv_halo[:2], far_q)
    ctx_3, ctx_2 = swap(ctx_far[0], 3), swap(ctx_far[1], 2)
    ctx_near = attend(rows, cols, (1, 0), (None, None), lengths, kv_group + kv_halo[2:], q_near)
    ctx_1 = swap(ctx_near[0], 1)

    def tail_of(part):
        tail = part[rows + EDGE : rows + 3 * EDGE]
        return jnp.concatenate([tail[:EDGE], tail[EDGE:]], axis=1)

    member = lax.axis_index("seq") % GROUP
    near_tail, diagonal, beyond = tail_of(kv_group[1]), tail_of(kv_group[3]), tail_of(kv_halo[3])
    other_tail = jnp.where((member == 0) | (member == GROUP - 1), beyond, diagonal)
    odd = member % 2 == 1
    before = jnp.where(odd, near_tail, other_tail)
    after = jnp.where(odd, other_tail, near_tail)

    around = (residual, before, after, depth_kernel)
    early = (0, 2, 3)
    mixed, conv = convolve_early(early, lengths, [ctx_near[1], ctx_2, ctx_3], *around)
    late = (1,)
    return finish(late, early, lengths, [ctx_1], *around, gain[None, :], shift[None, :], mixed, conv)


def solution(mesh):
    return jax.shard_map(
        local,
        mesh=mesh,
        in_specs=(
            P(("dp", "seq"), None),
            P(("dp", "seq"), None),
            P(("dp", "seq"), None),
            P(("dp", "seq"), None),
            P("dp"),
            P(),
            P(),
            P(),
        ),
        out_specs=P(("dp", "seq"), None),
        check_vma=False,
    )
```

```python
import functools

import jax
import jax.numpy as jnp
from jax import lax
from jax.experimental import pallas as pl
from jax.experimental.pallas import tpu as pltpu
from jax.sharding import PartitionSpec as P

HD = 64
LANES = 128
GROUP = 4
EDGE = 16
SAME = 2048.0
TAILED = (1, GROUP - 1)
WITH_Q = (3,)
KV_BLOCKS = GROUP + 2
WIDTHS = tuple(range(256, 1281, 128))
BLOCK_ROWS = 64
SPLIT_VMEM = 56 << 20
ATTEND_VMEM = 24 << 20
FINISH_VMEM = 24 << 20

ANY = pl.BlockSpec(memory_space=pl.ANY)
VMEM = pl.BlockSpec(memory_space=pltpu.VMEM)
SMEM = pl.BlockSpec(memory_space=pltpu.SMEM)


def group_place(rows):
    me = lax.axis_index("seq")
    member = me % GROUP
    return member, (me - member) * rows, [lax.bitwise_xor(member, m) for m in range(GROUP)]


def tail_rows(m):
    return 2 * EDGE if m in TAILED else 0


def split_kernel(cols, query, key, value, residual, *refs):
    kv_outs, q_outs = refs[:GROUP], refs[GROUP : 2 * GROUP - len(WITH_Q)]
    q_buf, kv_buf, edges, tail, in_sem, out_sem = refs[2 * GROUP - len(WITH_Q) :]
    rows = q_buf.shape[0]
    half = rows // 2
    _, _, which = group_place(rows)
    loads = []
    for i, (src, dst) in enumerate(((key, kv_buf.at[0]), (value, kv_buf.at[1]), (query, q_buf))):
        for part in range(2):
            at = pl.ds(part * half, half)
            sem = in_sem.at[2 * i + part]
            loads.append(pltpu.make_async_copy(src.at[at, :], dst.at[at, :], sem))
    for load in loads:
        load.start()
    tails = [None] * GROUP
    for m in TAILED:
        if m == 1:
            up = which[m] > which[0]
        else:
            up = (which[0] == 1) | (which[0] == GROUP - 1)
        at = pl.multiple_of(jnp.where(up, rows - EDGE, 0), EDGE)
        src = residual.at[pl.ds(at, EDGE), :]
        tails[m] = pltpu.make_async_copy(src, tail.at[m], in_sem.at[6 + m])
        tails[m].start()
    stores = []

    def store(src, dst):
        copy = pltpu.make_async_copy(src, dst, out_sem.at[len(stores)])
        copy.start()
        stores.append(copy)

    mine = [pl.ds(pl.multiple_of(which[m] * cols, LANES), cols) for m in range(GROUP)]
    for i in range(2):
        loads[2 * i].wait()
        loads[2 * i + 1].wait()
        for m in range(GROUP):
            store(kv_buf.at[i, :, mine[m]], kv_outs[m].at[pl.ds(0, rows), pl.ds(i * cols, cols)])
    loads[4].wait()
    loads[5].wait()
    q_alone = [m for m in range(GROUP) if m not in WITH_Q]
    for m in range(GROUP):
        edges[m, :, :cols] = q_buf[:EDGE, mine[m]]
        edges[m, :, cols:] = q_buf[rows - EDGE :, mine[m]]
        if m in WITH_Q:
            at = pl.ds(rows + EDGE + tail_rows(m), half)
            for part in range(2):
                src = q_buf.at[pl.ds(part * half, half), mine[m]]
                store(src, kv_outs[m].at[at, pl.ds(part * cols, cols)])
        else:
            store(q_buf.at[:, mine[m]], q_outs[q_alone.index(m)])
    for m in TAILED:
        tails[m].wait()
        for part in range(2):
            at = pl.ds(rows + (1 + part) * EDGE, EDGE)
            store(tail.at[m, :, pl.ds(part * 2 * cols, 2 * cols)], kv_outs[m].at[at, :])
    for m in range(GROUP):
        store(edges.at[m], kv_outs[m].at[pl.ds(rows, EDGE), :])
    for copy in stores:
        copy.wait()


def split_columns(query, key, value, residual):
    rows, width = query.shape
    cols = width // GROUP
    kind = query.dtype
    dma = pltpu.SemaphoreType.DMA
    sizes = [
        rows + EDGE + tail_rows(m) + (rows // 2 if m in WITH_Q else 0) for m in range(GROUP)
    ]
    n_alone = GROUP - len(WITH_Q)
    got = pl.pallas_call(
        functools.partial(split_kernel, cols),
        out_shape=[jax.ShapeDtypeStruct((size, 2 * cols), kind) for size in sizes]
        + [jax.ShapeDtypeStruct((rows, cols), kind)] * n_alone,
        in_specs=[ANY] * 4,
        out_specs=[ANY] * (GROUP + n_alone),
        scratch_shapes=[
            pltpu.VMEM((rows, width), kind),
            pltpu.VMEM((2, rows, width), kind),
            pltpu.VMEM((GROUP, EDGE, 2 * cols), kind),
            pltpu.VMEM((GROUP, EDGE, width), kind),
            dma((6 + GROUP,)),
            dma((4 * GROUP + 2 * len(TAILED) + len(WITH_Q),)),
        ],
        compiler_params=pltpu.CompilerParams(vmem_limit_bytes=SPLIT_VMEM),
        name="split_columns",
    )(query, key, value, residual)
    return got[:GROUP], got[GROUP:]


def attend_kernel(rows, q_rows, widths, ms, q_at, lengths, *refs):
    kv_in, q_in, outs = refs[:KV_BLOCKS], refs[KV_BLOCKS : KV_BLOCKS + 2], refs[KV_BLOCKS + 2 : KV_BLOCKS + 4]
    q_buf, kv_buf, oh_buf, edges, ctx_buf, q_sem, kv_sem, edge_sem, out_sem, meta = refs[
        KV_BLOCKS + 4 :
    ]
    cols = q_buf.shape[1]
    half = rows // 2
    blocks = ctx_buf.shape[1] // q_rows
    _, base, which = group_place(rows)
    pair = which[ms[0]] // 2
    key_base = base + (2 * pair - 2) * rows
    place = [w - 2 * pair + 2 for w in which]
    place += [which[m] % 2 + 4 * pair for m in range(GROUP) if m not in ms]
    place += [which[m] % 2 for m in ms]
    copies = []
    for i, src in enumerate(kv_in):
        at = pl.multiple_of(place[i] * rows, 16)
        src_rows = src.at[pl.ds(0, rows), :]
        copies.append(pltpu.make_async_copy(src_rows, kv_buf.at[pl.ds(at, rows), :], kv_sem.at[i]))
        src_rows = src.at[pl.ds(rows, EDGE), :]
        copies.append(pltpu.make_async_copy(src_rows, edges.at[place[i]], edge_sem.at[i]))
    for i, src in enumerate(q_in):
        at = pl.multiple_of(place[KV_BLOCKS + i] * rows + EDGE, 16)
        if q_at[i] is None:
            dst = q_buf.at[pl.ds(at, rows), :]
            copies.append(pltpu.make_async_copy(src, dst, q_sem.at[2 * i]))
        else:
            for part in range(2):
                part_of = src.at[pl.ds(q_at[i], half), pl.ds(part * cols, cols)]
                dst = q_buf.at[pl.ds(at + part * half, half), :]
                copies.append(pltpu.make_async_copy(part_of, dst, q_sem.at[2 * i + part]))
    for copy in copies:
        copy.start()

    utt_lane = lax.broadcasted_iota(jnp.int32, (1, oh_buf.shape[1]), 1)
    spans = []
    for m in ms:
        own = base + which[m] * rows
        spans += [(own, own + q_rows - EDGE - 1), (own + q_rows - EDGE, own + rows - 1)]

    def visit(u, carry):
        end, low_of, high_of, starts, ends = carry
        start, end = end, end + lengths[u]
        low_of = [jnp.where((a >= start) & (a < end), start, x) for (a, _), x in zip(spans, low_of)]
        high_of = [jnp.where((b >= start) & (b < end), end, x) for (_, b), x in zip(spans, high_of)]
        here = utt_lane == u
        return end, low_of, high_of, jnp.where(here, start, starts), jnp.where(here, end, ends)

    zero, none = jnp.int32(0), jnp.zeros(utt_lane.shape, jnp.int32)
    _, low_of, high_of, starts, ends = lax.fori_loop(
        0, lengths.shape[0], visit, (zero, [zero] * len(spans), [zero] * len(spans), none, none)
    )
    keys = kv_buf.shape[0]
    for t in range(len(spans)):
        low = jnp.maximum(low_of[t] - key_base, 0) // 16 * 16
        need = jnp.minimum(high_of[t] - key_base, keys) - low
        taken = widths[-1]
        for width in widths[-2::-1]:
            taken = jnp.where(need <= width, width, taken)
        meta[0, t] = jnp.minimum(low, keys - taken)
        meta[1, t] = need
        meta[2, t] = which[ms[t // blocks]] % 2 * rows + t % blocks * q_rows

    def one_hot(first, n, value):
        frame = first + lax.broadcasted_iota(jnp.int32, (n, utt_lane.shape[1]), 0)
        inside = (frame >= starts) & (frame < ends)
        return jnp.where(inside, jnp.float32(value), jnp.float32(0.0)).astype(jnp.bfloat16)

    @pl.loop(0, kv_buf.shape[0] // half)
    def _(i):
        at = pl.multiple_of(i * half, 16)
        oh_buf[pl.ds(at, half), :] = one_hot(key_base + at, half, 1.0)

    for copy in copies:
        copy.wait()
    q_buf[:EDGE, :] = edges[1, :, cols:]
    q_buf[EDGE + 2 * rows :, :] = edges[KV_BLOCKS - 2, :, :cols]

    lane = lax.broadcasted_iota(jnp.int32, (1, LANES), 1)
    scale = HD**-0.5
    halves = [
        jnp.where(lane // HD == h, jnp.float32(scale), jnp.float32(0.0)).astype(jnp.bfloat16)
        for h in range(2)
    ]

    def block(m, b, low, first, width):
        at = pl.multiple_of(b * q_rows, 16)
        oh_q = one_hot(key_base + 2 * rows - EDGE + first, q_rows, SAME)
        oh_k = oh_buf[pl.ds(low, width), :]
        oh_both = jnp.concatenate([oh_q, oh_q], axis=0)
        def scores(p_at):
            at_cols = slice(p_at, p_at + LANES)
            q = q_buf[pl.ds(first, q_rows), at_cols]
            k = jnp.concatenate([kv_buf[pl.ds(low, width), at_cols], oh_k], axis=1)
            q_both = jnp.concatenate([q * halves[0], q * halves[1]], axis=0)
            q_both = jnp.concatenate([q_both, oh_both], axis=1)
            return lax.dot_general(
                q_both, k, (((1,), (1,)), ((), ())), preferred_element_type=jnp.float32
            )

        def weigh(s, p_at):
            p = jnp.exp(s - jnp.max(s, axis=1, keepdims=True))
            return p.astype(jnp.bfloat16), jnp.sum(p, axis=1, keepdims=True)

        def combine(p, denom, p_at):
            v = kv_buf[pl.ds(low, width), cols + p_at : cols + p_at + LANES]
            o = jnp.dot(p, v, preferred_element_type=jnp.float32) / denom
            ctx = jnp.where(lane < HD, o[:q_rows], o[q_rows:])
            ctx_buf[m, pl.ds(at, q_rows), p_at : p_at + LANES] = ctx.astype(jnp.bfloat16)

        pairs = range(0, cols, LANES)
        got = [scores(p_at) for p_at in pairs]
        for p_at, s in zip(pairs, got):
            combine(*weigh(s, p_at), p_at)

    @pl.loop(0, 2 * blocks)
    def _(t):
        m, b = t // blocks, t % blocks
        low, need = pl.multiple_of(meta[0, t], 16), meta[1, t]
        first = pl.multiple_of(meta[2, t], 16)
        below = 0
        for width in widths:

            @pl.when((need > below) & (need <= width))
            def _(width=width):
                block(m, b, low, first, width)

            below = width

    copies = [pltpu.make_async_copy(ctx_buf.at[m], outs[m], out_sem.at[m]) for m in range(2)]
    for copy in copies:
        copy.start()
    for copy in copies:
        copy.wait()


def attend(rows, cols, ms, q_at, lengths, kv_parts, q_parts):
    keys = KV_BLOCKS * rows
    ext = rows + 2 * EDGE
    q_rows = ext // 2
    most = -(-(q_rows + 4 * rows + 16) // LANES) * LANES
    widths = sorted({min(w, most) for w in WIDTHS + (most,)})
    utts = -(-lengths.shape[0] // LANES) * LANES
    shape = jax.ShapeDtypeStruct((ext, cols), jnp.bfloat16)
    dma = pltpu.SemaphoreType.DMA
    return pl.pallas_call(
        functools.partial(attend_kernel, rows, q_rows, widths, ms, q_at),
        out_shape=[shape] * 2,
        in_specs=[SMEM] + [ANY] * (KV_BLOCKS + 2),
        out_specs=[ANY] * 2,
        scratch_shapes=[
            pltpu.VMEM((2 * rows + 2 * EDGE, cols), jnp.bfloat16),
            pltpu.VMEM((keys, 2 * cols), jnp.bfloat16),
            pltpu.VMEM((keys, utts), jnp.bfloat16),
            pltpu.VMEM((KV_BLOCKS, EDGE, 2 * cols), jnp.bfloat16),
            pltpu.VMEM((2, ext, cols), jnp.bfloat16),
            dma((4,)),
            dma((KV_BLOCKS,)),
            dma((KV_BLOCKS,)),
            dma((2,)),
            pltpu.SMEM((3, 4), jnp.int32),
        ],
        compiler_params=pltpu.CompilerParams(vmem_limit_bytes=ATTEND_VMEM),
        cost_estimate=pl.CostEstimate(
            flops=32 * ext * cols * keys, bytes_accessed=8 * keys * cols, transcendentals=0
        ),
        name="attend",
    )(lengths, *kv_parts, *q_parts)


def convolve(block_rows, ms, lengths, ctx_in, res, before, after, kernel, mixed_out, conv_out, scratch):
    mixed, window, starts, ends = scratch
    rows, width = res.shape
    _, base, which = group_place(rows)
    own = base + which[0] * rows
    per = width // LANES // GROUP
    taps = kernel.shape[0]
    half = taps // 2
    tiles = [
        (i, t, pl.ds(pl.multiple_of((which[m] * per + t) * LANES, LANES), LANES))
        for i, m in enumerate(ms)
        for t in range(per)
    ]

    def note(u, end):
        starts[u] = end
        ends[u] = end + lengths[u]
        return end + lengths[u]

    lax.fori_loop(0, lengths.shape[0], note, jnp.int32(0))
    for slot, (i, t, cols) in enumerate(tiles):
        ctx = ctx_in[i][:, t * LANES : (t + 1) * LANES].astype(jnp.float32)
        for first, part in ((0, before), (EDGE, res), (EDGE + rows, after)):
            at = slice(first, first + part.shape[0])
            total = (part[:, cols].astype(jnp.float32) + ctx[at]).astype(jnp.bfloat16)
            mixed[slot, at, :] = total.astype(jnp.float32)
            if part is res:
                mixed_out[slot] = total

    span = block_rows + 2 * EDGE

    def past(frame):
        return lambda u: ends[u] <= frame

    @pl.loop(0, rows // block_rows, init_carry=jnp.int32(0))
    def _(b, first_utt):
        top = pl.multiple_of(b * block_rows, 16)
        around = own + top - EDGE + lax.broadcasted_iota(jnp.int32, (span, LANES), 0)
        frame = own + top + lax.broadcasted_iota(jnp.int32, (block_rows, LANES), 0)
        first_utt = lax.while_loop(past(own + top), lambda u: u + 1, first_utt)
        last_utt = lax.while_loop(past(own + top + block_rows - 1), lambda u: u + 1, first_utt)

        @pl.loop(first_utt, last_utt + 1)
        def _(u):
            low, high = starts[u], ends[u]
            kept = (around >= low) & (around < high)
            mine = (frame >= low) & (frame < high)
            for slot in range(len(tiles)):
                window[slot] = jnp.where(kept, mixed[slot, pl.ds(top, span), :], jnp.float32(0.0))
            for slot, (_, _, cols) in enumerate(tiles):
                total = jnp.zeros((block_rows, LANES), jnp.float32)
                for tap in range(taps):
                    at = tap + EDGE - half
                    total = total + window[slot, at : at + block_rows, :] * kernel[tap : tap + 1, cols]
                at = pl.ds(top, block_rows)
                conv_out[slot, at, :] = jnp.where(mine, total, conv_out[slot, at, :])

        return last_utt


def convolve_kernel(block_rows, ms, lengths, *refs):
    ctx_in = refs[: len(ms)]
    res, before, after, kernel, mixed_out, conv_out = refs[len(ms) : len(ms) + 6]
    scratch = refs[len(ms) + 6 :]
    convolve(block_rows, ms, lengths, ctx_in, res, before, after, kernel, mixed_out, conv_out, scratch)


def finish_kernel(block_rows, ms, early, lengths, *refs):
    ctx_in = refs[: len(ms)]
    res, before, after, kernel, gain, shift, mixed_in, conv_in, out = refs[len(ms) : len(ms) + 9]
    mixed_own, conv_own = refs[len(ms) + 9 : len(ms) + 11]
    scratch = refs[len(ms) + 11 :]
    convolve(block_rows, ms, lengths, ctx_in, res, before, after, kernel, mixed_own, conv_own, scratch)
    rows, width = res.shape
    _, _, which = group_place(rows)
    per = width // LANES // GROUP
    sources = []
    for group, mixed, conv in ((early, mixed_in, conv_in), (ms, mixed_own, conv_own)):
        for i, m in enumerate(group):
            for t in range(per):
                cols = pl.ds(pl.multiple_of((which[m] * per + t) * LANES, LANES), LANES)
                sources.append((mixed, conv, i * per + t, cols))

    norm_rows = rows // 2

    @pl.loop(0, 2)
    def _(b):
        at = pl.ds(pl.multiple_of(b * norm_rows, 16), norm_rows)
        values = [conv[slot, at, :] for _, conv, slot, _ in sources]
        mean = jnp.sum(sum(values), axis=1, keepdims=True) / width
        centred = [x - mean for x in values]
        var = jnp.sum(sum([x * x for x in centred]), axis=1, keepdims=True) / width
        inverse = 1.0 / jnp.sqrt(var + 1e-05)
        for x, (mixed, _, slot, cols) in zip(centred, sources):
            normed = x * inverse * gain[:, cols] + shift[:, cols]
            gated = normed * jax.nn.sigmoid(normed)
            out[at, cols] = (mixed[slot, at, :].astype(jnp.float32) + gated).astype(jnp.bfloat16)


def conv_scratch(slots, rows, block_rows, utts):
    return [
        pltpu.VMEM((slots, rows + 2 * EDGE, LANES), jnp.float32),
        pltpu.VMEM((slots, block_rows + 2 * EDGE, LANES), jnp.float32),
        pltpu.SMEM((utts,), jnp.int32),
        pltpu.SMEM((utts,), jnp.int32),
    ]


def convolve_early(ms, lengths, ctx_parts, res, before, after, kernel):
    rows, width = res.shape
    slots = len(ms) * width // LANES // GROUP
    taps = kernel.shape[0]
    return pl.pallas_call(
        functools.partial(convolve_kernel, BLOCK_ROWS, ms),
        out_shape=[
            jax.ShapeDtypeStruct((slots, rows, LANES), jnp.bfloat16),
            jax.ShapeDtypeStruct((slots, rows, LANES), jnp.float32),
        ],
        in_specs=[SMEM] + [VMEM] * (len(ms) + 4),
        out_specs=[VMEM] * 2,
        scratch_shapes=conv_scratch(slots, rows, BLOCK_ROWS, lengths.shape[0]),
        compiler_params=pltpu.CompilerParams(vmem_limit_bytes=FINISH_VMEM),
        cost_estimate=pl.CostEstimate(
            flops=100 * taps * rows * slots * LANES, bytes_accessed=8 * rows * width, transcendentals=0
        ),
        name="convolve",
    )(lengths, *ctx_parts, res, before, after, kernel)


def finish(ms, early, lengths, ctx_parts, res, before, after, kernel, gain, shift, mixed, conv):
    rows, width = res.shape
    slots = len(ms) * width // LANES // GROUP
    return pl.pallas_call(
        functools.partial(finish_kernel, BLOCK_ROWS, ms, early),
        out_shape=jax.ShapeDtypeStruct((rows, width), jnp.bfloat16),
        in_specs=[SMEM] + [VMEM] * (len(ms) + 8),
        out_specs=VMEM,
        scratch_shapes=[
            pltpu.VMEM((slots, rows, LANES), jnp.bfloat16),
            pltpu.VMEM((slots, rows, LANES), jnp.float32),
        ]
        + conv_scratch(slots, rows, BLOCK_ROWS, lengths.shape[0]),
        compiler_params=pltpu.CompilerParams(vmem_limit_bytes=FINISH_VMEM),
        name="finish",
    )(lengths, *ctx_parts, res, before, after, kernel, gain, shift, mixed, conv)


def local(query, key, value, residual, lengths, depth_kernel, gain, shift):
    rows, width = query.shape
    cols = width // GROUP
    peers = lax.axis_size("seq")

    def swap(array, m):
        return lax.ppermute(array, "seq", [(i, i ^ m) for i in range(peers)])

    def move(array, by):
        pairs = [(i, i + by(i)) for i in range(peers)]
        return lax.ppermute(array, "seq", [(i, j) for i, j in pairs if 0 <= j < peers])

    near = lambda i: -GROUP if i % GROUP < GROUP // 2 else GROUP
    far = lambda i: -near(i)

    kv, q_alone = split_columns(query, key, value, residual)
    kv_group = [kv[0]] + [swap(kv[m], m) for m in range(1, GROUP)]
    q_1, q_2, kv_group[1] = lax.optimization_barrier((*q_alone[1:], kv_group[1]))
    q_2 = swap(q_2, 2)
    q_1, kv_group[2] = lax.optimization_barrier((q_1, kv_group[2]))
    q_near = [swap(q_1, 1), q_alone[0]]
    bare = [part[: rows + EDGE + tail_rows(m)] for m, part in enumerate(kv_group)]
    kv_halo = [move(bare[m], near) for m in range(2)]
    both = move(jnp.concatenate(bare[2:], axis=0), far)
    kv_halo += [both[: bare[2].shape[0]], both[bare[2].shape[0] :]]

    q_at = (rows + EDGE + tail_rows(3), None)
    far_q = [kv_group[3], q_2]
    ctx_far = attend(rows, cols, (3, 2), q_at, lengths, kv_group + kv_halo[:2], far_q)
    ctx_3, ctx_2 = swap(ctx_far[0], 3), swap(ctx_far[1], 2)
    ctx_near = attend(rows, cols, (1, 0), (None, None), lengths, kv_group + kv_halo[2:], q_near)
    ctx_1 = swap(ctx_near[0], 1)

    def tail_of(part):
        tail = part[rows + EDGE : rows + 3 * EDGE]
        return jnp.concatenate([tail[:EDGE], tail[EDGE:]], axis=1)

    member = lax.axis_index("seq") % GROUP
    near_tail, diagonal, beyond = tail_of(kv_group[1]), tail_of(kv_group[3]), tail_of(kv_halo[3])
    other_tail = jnp.where((member == 0) | (member == GROUP - 1), beyond, diagonal)
    odd = member % 2 == 1
    before = jnp.where(odd, near_tail, other_tail)
    after = jnp.where(odd, other_tail, near_tail)

    around = (residual, before, after, depth_kernel)
    early = (0, 2, 3)
    mixed, conv = convolve_early(early, lengths, [ctx_near[1], ctx_2, ctx_3], *around)
    late = (1,)
    return finish(late, early, lengths, [ctx_1], *around, gain[None, :], shift[None, :], mixed, conv)


def solution(mesh):
    return jax.shard_map(
        local,
        mesh=mesh,
        in_specs=(
            P(("dp", "seq"), None),
            P(("dp", "seq"), None),
            P(("dp", "seq"), None),
            P(("dp", "seq"), None),
            P("dp"),
            P(),
            P(),
            P(),
        ),
        out_specs=P(("dp", "seq"), None),
        check_vma=False,
    )
```

```python
import functools

import jax
import jax.numpy as jnp
from jax import lax
from jax.experimental import pallas as pl
from jax.experimental.pallas import tpu as pltpu
from jax.sharding import PartitionSpec as P

HD = 64
LANES = 128
GROUP = 4
EDGE = 16
SAME = 2048.0
TAILED = (1, GROUP - 1)
WITH_Q = ()
KV_BLOCKS = GROUP + 2
WIDTHS = tuple(range(256, 1281, 128))
BLOCK_ROWS = 64
SPLIT_VMEM = 56 << 20
ATTEND_VMEM = 24 << 20
FINISH_VMEM = 24 << 20

ANY = pl.BlockSpec(memory_space=pl.ANY)
VMEM = pl.BlockSpec(memory_space=pltpu.VMEM)
SMEM = pl.BlockSpec(memory_space=pltpu.SMEM)


def group_place(rows):
    me = lax.axis_index("seq")
    member = me % GROUP
    return member, (me - member) * rows, [lax.bitwise_xor(member, m) for m in range(GROUP)]


def tail_rows(m):
    return 2 * EDGE if m in TAILED else 0


def split_kernel(cols, query, key, value, residual, *refs):
    kv_outs, q_outs = refs[:GROUP], refs[GROUP : 2 * GROUP - len(WITH_Q)]
    q_buf, kv_buf, edges, tail, in_sem, out_sem = refs[2 * GROUP - len(WITH_Q) :]
    rows = q_buf.shape[0]
    half = rows // 2
    _, _, which = group_place(rows)
    loads = []
    for i, (src, dst) in enumerate(((key, kv_buf.at[0]), (value, kv_buf.at[1]), (query, q_buf))):
        for part in range(2):
            at = pl.ds(part * half, half)
            sem = in_sem.at[2 * i + part]
            loads.append(pltpu.make_async_copy(src.at[at, :], dst.at[at, :], sem))
    for load in loads:
        load.start()
    tails = [None] * GROUP
    for m in TAILED:
        if m == 1:
            up = which[m] > which[0]
        else:
            up = (which[0] == 1) | (which[0] == GROUP - 1)
        at = pl.multiple_of(jnp.where(up, rows - EDGE, 0), EDGE)
        src = residual.at[pl.ds(at, EDGE), :]
        tails[m] = pltpu.make_async_copy(src, tail.at[m], in_sem.at[6 + m])
        tails[m].start()
    stores = []

    def store(src, dst):
        copy = pltpu.make_async_copy(src, dst, out_sem.at[len(stores)])
        copy.start()
        stores.append(copy)

    mine = [pl.ds(pl.multiple_of(which[m] * cols, LANES), cols) for m in range(GROUP)]
    for i in range(2):
        loads[2 * i].wait()
        loads[2 * i + 1].wait()
        for m in range(GROUP):
            store(kv_buf.at[i, :, mine[m]], kv_outs[m].at[pl.ds(0, rows), pl.ds(i * cols, cols)])
    loads[4].wait()
    loads[5].wait()
    q_alone = [m for m in range(GROUP) if m not in WITH_Q]
    for m in range(GROUP):
        edges[m, :, :cols] = q_buf[:EDGE, mine[m]]
        edges[m, :, cols:] = q_buf[rows - EDGE :, mine[m]]
        if m in WITH_Q:
            at = pl.ds(rows + EDGE + tail_rows(m), half)
            for part in range(2):
                src = q_buf.at[pl.ds(part * half, half), mine[m]]
                store(src, kv_outs[m].at[at, pl.ds(part * cols, cols)])
        else:
            store(q_buf.at[:, mine[m]], q_outs[q_alone.index(m)])
    for m in TAILED:
        tails[m].wait()
        for part in range(2):
            at = pl.ds(rows + (1 + part) * EDGE, EDGE)
            store(tail.at[m, :, pl.ds(part * 2 * cols, 2 * cols)], kv_outs[m].at[at, :])
    for m in range(GROUP):
        store(edges.at[m], kv_outs[m].at[pl.ds(rows, EDGE), :])
    for copy in stores:
        copy.wait()


def split_columns(query, key, value, residual):
    rows, width = query.shape
    cols = width // GROUP
    kind = query.dtype
    dma = pltpu.SemaphoreType.DMA
    sizes = [
        rows + EDGE + tail_rows(m) + (rows // 2 if m in WITH_Q else 0) for m in range(GROUP)
    ]
    n_alone = GROUP - len(WITH_Q)
    got = pl.pallas_call(
        functools.partial(split_kernel, cols),
        out_shape=[jax.ShapeDtypeStruct((size, 2 * cols), kind) for size in sizes]
        + [jax.ShapeDtypeStruct((rows, cols), kind)] * n_alone,
        in_specs=[ANY] * 4,
        out_specs=[ANY] * (GROUP + n_alone),
        scratch_shapes=[
            pltpu.VMEM((rows, width), kind),
            pltpu.VMEM((2, rows, width), kind),
            pltpu.VMEM((GROUP, EDGE, 2 * cols), kind),
            pltpu.VMEM((GROUP, EDGE, width), kind),
            dma((6 + GROUP,)),
            dma((4 * GROUP + 2 * len(TAILED) + len(WITH_Q),)),
        ],
        compiler_params=pltpu.CompilerParams(vmem_limit_bytes=SPLIT_VMEM),
        name="split_columns",
    )(query, key, value, residual)
    return got[:GROUP], got[GROUP:]


def attend_kernel(rows, q_rows, widths, ms, q_at, lengths, *refs):
    kv_in, q_in, outs = refs[:KV_BLOCKS], refs[KV_BLOCKS : KV_BLOCKS + 2], refs[KV_BLOCKS + 2 : KV_BLOCKS + 4]
    q_buf, kv_buf, oh_buf, edges, ctx_buf, q_sem, kv_sem, edge_sem, out_sem, meta = refs[
        KV_BLOCKS + 4 :
    ]
    cols = q_buf.shape[1]
    half = rows // 2
    blocks = ctx_buf.shape[1] // q_rows
    _, base, which = group_place(rows)
    pair = which[ms[0]] // 2
    key_base = base + (2 * pair - 2) * rows
    place = [w - 2 * pair + 2 for w in which]
    place += [which[m] % 2 + 4 * pair for m in range(GROUP) if m not in ms]
    place += [which[m] % 2 for m in ms]
    copies = []
    for i, src in enumerate(kv_in):
        at = pl.multiple_of(place[i] * rows, 16)
        src_rows = src.at[pl.ds(0, rows), :]
        copies.append(pltpu.make_async_copy(src_rows, kv_buf.at[pl.ds(at, rows), :], kv_sem.at[i]))
        src_rows = src.at[pl.ds(rows, EDGE), :]
        copies.append(pltpu.make_async_copy(src_rows, edges.at[place[i]], edge_sem.at[i]))
    for i, src in enumerate(q_in):
        at = pl.multiple_of(place[KV_BLOCKS + i] * rows + EDGE, 16)
        if q_at[i] is None:
            dst = q_buf.at[pl.ds(at, rows), :]
            copies.append(pltpu.make_async_copy(src, dst, q_sem.at[2 * i]))
        else:
            for part in range(2):
                part_of = src.at[pl.ds(q_at[i], half), pl.ds(part * cols, cols)]
                dst = q_buf.at[pl.ds(at + part * half, half), :]
                copies.append(pltpu.make_async_copy(part_of, dst, q_sem.at[2 * i + part]))
    for copy in copies:
        copy.start()

    utt_lane = lax.broadcasted_iota(jnp.int32, (1, oh_buf.shape[1]), 1)
    spans = []
    for m in ms:
        own = base + which[m] * rows
        spans += [(own, own + q_rows - EDGE - 1), (own + q_rows - EDGE, own + rows - 1)]

    def visit(u, carry):
        end, low_of, high_of, starts, ends = carry
        start, end = end, end + lengths[u]
        low_of = [jnp.where((a >= start) & (a < end), start, x) for (a, _), x in zip(spans, low_of)]
        high_of = [jnp.where((b >= start) & (b < end), end, x) for (_, b), x in zip(spans, high_of)]
        here = utt_lane == u
        return end, low_of, high_of, jnp.where(here, start, starts), jnp.where(here, end, ends)

    zero, none = jnp.int32(0), jnp.zeros(utt_lane.shape, jnp.int32)
    _, low_of, high_of, starts, ends = lax.fori_loop(
        0, lengths.shape[0], visit, (zero, [zero] * len(spans), [zero] * len(spans), none, none)
    )
    keys = kv_buf.shape[0]
    for t in range(len(spans)):
        low = jnp.maximum(low_of[t] - key_base, 0) // 16 * 16
        need = jnp.minimum(high_of[t] - key_base, keys) - low
        taken = widths[-1]
        for width in widths[-2::-1]:
            taken = jnp.where(need <= width, width, taken)
        meta[0, t] = jnp.minimum(low, keys - taken)
        meta[1, t] = need
        meta[2, t] = which[ms[t // blocks]] % 2 * rows + t % blocks * q_rows

    def one_hot(first, n, value):
        frame = first + lax.broadcasted_iota(jnp.int32, (n, utt_lane.shape[1]), 0)
        inside = (frame >= starts) & (frame < ends)
        return jnp.where(inside, jnp.float32(value), jnp.float32(0.0)).astype(jnp.bfloat16)

    @pl.loop(0, kv_buf.shape[0] // half)
    def _(i):
        at = pl.multiple_of(i * half, 16)
        oh_buf[pl.ds(at, half), :] = one_hot(key_base + at, half, 1.0)

    for copy in copies:
        copy.wait()
    q_buf[:EDGE, :] = edges[1, :, cols:]
    q_buf[EDGE + 2 * rows :, :] = edges[KV_BLOCKS - 2, :, :cols]

    lane = lax.broadcasted_iota(jnp.int32, (1, LANES), 1)
    scale = HD**-0.5
    halves = [
        jnp.where(lane // HD == h, jnp.float32(scale), jnp.float32(0.0)).astype(jnp.bfloat16)
        for h in range(2)
    ]

    def block(m, b, low, first, width):
        at = pl.multiple_of(b * q_rows, 16)
        oh_q = one_hot(key_base + 2 * rows - EDGE + first, q_rows, SAME)
        oh_k = oh_buf[pl.ds(low, width), :]
        oh_both = jnp.concatenate([oh_q, oh_q], axis=0)
        def scores(p_at):
            at_cols = slice(p_at, p_at + LANES)
            q = q_buf[pl.ds(first, q_rows), at_cols]
            k = jnp.concatenate([kv_buf[pl.ds(low, width), at_cols], oh_k], axis=1)
            q_both = jnp.concatenate([q * halves[0], q * halves[1]], axis=0)
            q_both = jnp.concatenate([q_both, oh_both], axis=1)
            return lax.dot_general(
                q_both, k, (((1,), (1,)), ((), ())), preferred_element_type=jnp.float32
            )

        def weigh(s, p_at):
            p = jnp.exp(s - jnp.max(s, axis=1, keepdims=True))
            return p.astype(jnp.bfloat16), jnp.sum(p, axis=1, keepdims=True)

        def combine(p, denom, p_at):
            v = kv_buf[pl.ds(low, width), cols + p_at : cols + p_at + LANES]
            o = jnp.dot(p, v, preferred_element_type=jnp.float32) / denom
            ctx = jnp.where(lane < HD, o[:q_rows], o[q_rows:])
            ctx_buf[m, pl.ds(at, q_rows), p_at : p_at + LANES] = ctx.astype(jnp.bfloat16)

        pairs = range(0, cols, LANES)
        got = [scores(p_at) for p_at in pairs]
        for p_at, s in zip(pairs, got):
            combine(*weigh(s, p_at), p_at)

    @pl.loop(0, 2 * blocks)
    def _(t):
        m, b = t // blocks, t % blocks
        low, need = pl.multiple_of(meta[0, t], 16), meta[1, t]
        first = pl.multiple_of(meta[2, t], 16)
        below = 0
        for width in widths:

            @pl.when((need > below) & (need <= width))
            def _(width=width):
                block(m, b, low, first, width)

            below = width

    copies = [pltpu.make_async_copy(ctx_buf.at[m], outs[m], out_sem.at[m]) for m in range(2)]
    for copy in copies:
        copy.start()
    for copy in copies:
        copy.wait()


def attend(rows, cols, ms, q_at, lengths, kv_parts, q_parts):
    keys = KV_BLOCKS * rows
    ext = rows + 2 * EDGE
    q_rows = ext // 2
    most = -(-(q_rows + 4 * rows + 16) // LANES) * LANES
    widths = sorted({min(w, most) for w in WIDTHS + (most,)})
    utts = -(-lengths.shape[0] // LANES) * LANES
    shape = jax.ShapeDtypeStruct((ext, cols), jnp.bfloat16)
    dma = pltpu.SemaphoreType.DMA
    return pl.pallas_call(
        functools.partial(attend_kernel, rows, q_rows, widths, ms, q_at),
        out_shape=[shape] * 2,
        in_specs=[SMEM] + [ANY] * (KV_BLOCKS + 2),
        out_specs=[ANY] * 2,
        scratch_shapes=[
            pltpu.VMEM((2 * rows + 2 * EDGE, cols), jnp.bfloat16),
            pltpu.VMEM((keys, 2 * cols), jnp.bfloat16),
            pltpu.VMEM((keys, utts), jnp.bfloat16),
            pltpu.VMEM((KV_BLOCKS, EDGE, 2 * cols), jnp.bfloat16),
            pltpu.VMEM((2, ext, cols), jnp.bfloat16),
            dma((4,)),
            dma((KV_BLOCKS,)),
            dma((KV_BLOCKS,)),
            dma((2,)),
            pltpu.SMEM((3, 4), jnp.int32),
        ],
        compiler_params=pltpu.CompilerParams(vmem_limit_bytes=ATTEND_VMEM),
        cost_estimate=pl.CostEstimate(
            flops=32 * ext * cols * keys, bytes_accessed=8 * keys * cols, transcendentals=0
        ),
        name="attend",
    )(lengths, *kv_parts, *q_parts)


def convolve(block_rows, ms, lengths, ctx_in, res, before, after, kernel, mixed_out, conv_out, scratch):
    mixed, window, starts, ends = scratch
    rows, width = res.shape
    _, base, which = group_place(rows)
    own = base + which[0] * rows
    per = width // LANES // GROUP
    taps = kernel.shape[0]
    half = taps // 2
    tiles = [
        (i, t, pl.ds(pl.multiple_of((which[m] * per + t) * LANES, LANES), LANES))
        for i, m in enumerate(ms)
        for t in range(per)
    ]

    def note(u, end):
        starts[u] = end
        ends[u] = end + lengths[u]
        return end + lengths[u]

    lax.fori_loop(0, lengths.shape[0], note, jnp.int32(0))
    for slot, (i, t, cols) in enumerate(tiles):
        ctx = ctx_in[i][:, t * LANES : (t + 1) * LANES].astype(jnp.float32)
        for first, part in ((0, before), (EDGE, res), (EDGE + rows, after)):
            at = slice(first, first + part.shape[0])
            total = (part[:, cols].astype(jnp.float32) + ctx[at]).astype(jnp.bfloat16)
            mixed[slot, at, :] = total.astype(jnp.float32)
            if part is res:
                mixed_out[slot] = total

    span = block_rows + 2 * EDGE

    def past(frame):
        return lambda u: ends[u] <= frame

    @pl.loop(0, rows // block_rows, init_carry=jnp.int32(0))
    def _(b, first_utt):
        top = pl.multiple_of(b * block_rows, 16)
        around = own + top - EDGE + lax.broadcasted_iota(jnp.int32, (span, LANES), 0)
        frame = own + top + lax.broadcasted_iota(jnp.int32, (block_rows, LANES), 0)
        first_utt = lax.while_loop(past(own + top), lambda u: u + 1, first_utt)
        last_utt = lax.while_loop(past(own + top + block_rows - 1), lambda u: u + 1, first_utt)

        @pl.loop(first_utt, last_utt + 1)
        def _(u):
            low, high = starts[u], ends[u]
            kept = (around >= low) & (around < high)
            mine = (frame >= low) & (frame < high)
            for slot in range(len(tiles)):
                window[slot] = jnp.where(kept, mixed[slot, pl.ds(top, span), :], jnp.float32(0.0))
            for slot, (_, _, cols) in enumerate(tiles):
                total = jnp.zeros((block_rows, LANES), jnp.float32)
                for tap in range(taps):
                    at = tap + EDGE - half
                    total = total + window[slot, at : at + block_rows, :] * kernel[tap : tap + 1, cols]
                at = pl.ds(top, block_rows)
                conv_out[slot, at, :] = jnp.where(mine, total, conv_out[slot, at, :])

        return last_utt


def convolve_kernel(block_rows, ms, lengths, *refs):
    ctx_in = refs[: len(ms)]
    res, before, after, kernel, mixed_out, conv_out = refs[len(ms) : len(ms) + 6]
    scratch = refs[len(ms) + 6 :]
    convolve(block_rows, ms, lengths, ctx_in, res, before, after, kernel, mixed_out, conv_out, scratch)


def finish_kernel(block_rows, ms, early, lengths, *refs):
    ctx_in = refs[: len(ms)]
    res, before, after, kernel, gain, shift, mixed_in, conv_in, out = refs[len(ms) : len(ms) + 9]
    mixed_own, conv_own = refs[len(ms) + 9 : len(ms) + 11]
    scratch = refs[len(ms) + 11 :]
    convolve(block_rows, ms, lengths, ctx_in, res, before, after, kernel, mixed_own, conv_own, scratch)
    rows, width = res.shape
    _, _, which = group_place(rows)
    per = width // LANES // GROUP
    sources = []
    for group, mixed, conv in ((early, mixed_in, conv_in), (ms, mixed_own, conv_own)):
        for i, m in enumerate(group):
            for t in range(per):
                cols = pl.ds(pl.multiple_of((which[m] * per + t) * LANES, LANES), LANES)
                sources.append((mixed, conv, i * per + t, cols))

    norm_rows = rows // 2

    @pl.loop(0, 2)
    def _(b):
        at = pl.ds(pl.multiple_of(b * norm_rows, 16), norm_rows)
        values = [conv[slot, at, :] for _, conv, slot, _ in sources]
        mean = jnp.sum(sum(values), axis=1, keepdims=True) / width
        centred = [x - mean for x in values]
        var = jnp.sum(sum([x * x for x in centred]), axis=1, keepdims=True) / width
        inverse = 1.0 / jnp.sqrt(var + 1e-05)
        for x, (mixed, _, slot, cols) in zip(centred, sources):
            normed = x * inverse * gain[:, cols] + shift[:, cols]
            gated = normed * jax.nn.sigmoid(normed)
            out[at, cols] = (mixed[slot, at, :].astype(jnp.float32) + gated).astype(jnp.bfloat16)


def conv_scratch(slots, rows, block_rows, utts):
    return [
        pltpu.VMEM((slots, rows + 2 * EDGE, LANES), jnp.float32),
        pltpu.VMEM((slots, block_rows + 2 * EDGE, LANES), jnp.float32),
        pltpu.SMEM((utts,), jnp.int32),
        pltpu.SMEM((utts,), jnp.int32),
    ]


def convolve_early(ms, lengths, ctx_parts, res, before, after, kernel):
    rows, width = res.shape
    slots = len(ms) * width // LANES // GROUP
    taps = kernel.shape[0]
    return pl.pallas_call(
        functools.partial(convolve_kernel, BLOCK_ROWS, ms),
        out_shape=[
            jax.ShapeDtypeStruct((slots, rows, LANES), jnp.bfloat16),
            jax.ShapeDtypeStruct((slots, rows, LANES), jnp.float32),
        ],
        in_specs=[SMEM] + [VMEM] * (len(ms) + 4),
        out_specs=[VMEM] * 2,
        scratch_shapes=conv_scratch(slots, rows, BLOCK_ROWS, lengths.shape[0]),
        compiler_params=pltpu.CompilerParams(vmem_limit_bytes=FINISH_VMEM),
        cost_estimate=pl.CostEstimate(
            flops=100 * taps * rows * slots * LANES, bytes_accessed=8 * rows * width, transcendentals=0
        ),
        name="convolve",
    )(lengths, *ctx_parts, res, before, after, kernel)


def finish(ms, early, lengths, ctx_parts, res, before, after, kernel, gain, shift, mixed, conv):
    rows, width = res.shape
    slots = len(ms) * width // LANES // GROUP
    return pl.pallas_call(
        functools.partial(finish_kernel, BLOCK_ROWS, ms, early),
        out_shape=jax.ShapeDtypeStruct((rows, width), jnp.bfloat16),
        in_specs=[SMEM] + [VMEM] * (len(ms) + 8),
        out_specs=VMEM,
        scratch_shapes=[
            pltpu.VMEM((slots, rows, LANES), jnp.bfloat16),
            pltpu.VMEM((slots, rows, LANES), jnp.float32),
        ]
        + conv_scratch(slots, rows, BLOCK_ROWS, lengths.shape[0]),
        compiler_params=pltpu.CompilerParams(vmem_limit_bytes=FINISH_VMEM),
        name="finish",
    )(lengths, *ctx_parts, res, before, after, kernel, gain, shift, mixed, conv)


def local(query, key, value, residual, lengths, depth_kernel, gain, shift):
    rows, width = query.shape
    cols = width // GROUP
    peers = lax.axis_size("seq")

    def swap(array, m):
        return lax.ppermute(array, "seq", [(i, i ^ m) for i in range(peers)])

    def move(array, by):
        pairs = [(i, i + by(i)) for i in range(peers)]
        return lax.ppermute(array, "seq", [(i, j) for i, j in pairs if 0 <= j < peers])

    near = lambda i: -GROUP if i % GROUP < GROUP // 2 else GROUP
    far = lambda i: -near(i)

    kv, q_alone = split_columns(query, key, value, residual)
    kv_group = [kv[0]] + [swap(kv[m], m) for m in range(1, GROUP)]
    q_2, q_3, kv_group[1] = lax.optimization_barrier((*q_alone[2:], kv_group[1]))
    q_3, q_2 = swap(q_3, 3), swap(q_2, 2)
    q_1, kv_group[3] = lax.optimization_barrier((q_alone[1], kv_group[3]))
    q_near = [swap(q_1, 1), q_alone[0]]
    bare = [part[: rows + EDGE + tail_rows(m)] for m, part in enumerate(kv_group)]
    kv_halo = [move(bare[m], near) for m in range(2)]
    both = move(jnp.concatenate(bare[2:], axis=0), far)
    kv_halo += [both[: bare[2].shape[0]], both[bare[2].shape[0] :]]

    q_at = (None, None)
    far_q = [q_3, q_2]
    ctx_far = attend(rows, cols, (3, 2), q_at, lengths, kv_group + kv_halo[:2], far_q)
    ctx_3, ctx_2 = swap(ctx_far[0], 3), swap(ctx_far[1], 2)
    ctx_near = attend(rows, cols, (1, 0), (None, None), lengths, kv_group + kv_halo[2:], q_near)
    ctx_1 = swap(ctx_near[0], 1)

    def tail_of(part):
        tail = part[rows + EDGE : rows + 3 * EDGE]
        return jnp.concatenate([tail[:EDGE], tail[EDGE:]], axis=1)

    member = lax.axis_index("seq") % GROUP
    near_tail, diagonal, beyond = tail_of(kv_group[1]), tail_of(kv_group[3]), tail_of(kv_halo[3])
    other_tail = jnp.where((member == 0) | (member == GROUP - 1), beyond, diagonal)
    odd = member % 2 == 1
    before = jnp.where(odd, near_tail, other_tail)
    after = jnp.where(odd, other_tail, near_tail)

    around = (residual, before, after, depth_kernel)
    early = (0, 2, 3)
    mixed, conv = convolve_early(early, lengths, [ctx_near[1], ctx_2, ctx_3], *around)
    late = (1,)
    return finish(late, early, lengths, [ctx_1], *around, gain[None, :], shift[None, :], mixed, conv)


def solution(mesh):
    return jax.shard_map(
        local,
        mesh=mesh,
        in_specs=(
            P(("dp", "seq"), None),
            P(("dp", "seq"), None),
            P(("dp", "seq"), None),
            P(("dp", "seq"), None),
            P("dp"),
            P(),
            P(),
            P(),
        ),
        out_specs=P(("dp", "seq"), None),
        check_vma=False,
    )
```

```python
import functools

import jax
import jax.numpy as jnp
from jax import lax
from jax.experimental import pallas as pl
from jax.experimental.pallas import tpu as pltpu
from jax.sharding import PartitionSpec as P

HD = 64
LANES = 128
GROUP = 4
EDGE = 16
SAME = 2048.0
TAILED = (0, 1)
WITH_Q = ()
KV_BLOCKS = GROUP + 2
WIDTHS = tuple(range(256, 1281, 128))
BLOCK_ROWS = 64
SPLIT_VMEM = 56 << 20
ATTEND_VMEM = 24 << 20
FINISH_VMEM = 24 << 20

ANY = pl.BlockSpec(memory_space=pl.ANY)
VMEM = pl.BlockSpec(memory_space=pltpu.VMEM)
SMEM = pl.BlockSpec(memory_space=pltpu.SMEM)


def group_place(rows):
    me = lax.axis_index("seq")
    member = me % GROUP
    return member, (me - member) * rows, [lax.bitwise_xor(member, m) for m in range(GROUP)]


def tail_rows(m):
    return 2 * EDGE if m in TAILED else 0


def split_kernel(cols, query, key, value, residual, *refs):
    kv_outs, q_outs = refs[:GROUP], refs[GROUP : 2 * GROUP - len(WITH_Q)]
    q_buf, kv_buf, edges, tail, in_sem, out_sem = refs[2 * GROUP - len(WITH_Q) :]
    rows = q_buf.shape[0]
    half = rows // 2
    _, _, which = group_place(rows)
    loads = []
    for i, (src, dst) in enumerate(((key, kv_buf.at[0]), (value, kv_buf.at[1]), (query, q_buf))):
        for part in range(2):
            at = pl.ds(part * half, half)
            sem = in_sem.at[2 * i + part]
            loads.append(pltpu.make_async_copy(src.at[at, :], dst.at[at, :], sem))
    for load in loads:
        load.start()
    tails = [None] * GROUP
    for m in TAILED:
        up = which[m] > which[0] if m else which[0] % 2 == 1
        at = pl.multiple_of(jnp.where(up, rows - EDGE, 0), EDGE)
        src = residual.at[pl.ds(at, EDGE), :]
        tails[m] = pltpu.make_async_copy(src, tail.at[m], in_sem.at[6 + m])
        tails[m].start()
    stores = []

    def store(src, dst):
        copy = pltpu.make_async_copy(src, dst, out_sem.at[len(stores)])
        copy.start()
        stores.append(copy)

    mine = [pl.ds(pl.multiple_of(which[m] * cols, LANES), cols) for m in range(GROUP)]
    for i in range(2):
        loads[2 * i].wait()
        loads[2 * i + 1].wait()
        for m in range(GROUP):
            store(kv_buf.at[i, :, mine[m]], kv_outs[m].at[pl.ds(0, rows), pl.ds(i * cols, cols)])
    loads[4].wait()
    loads[5].wait()
    q_alone = [m for m in range(GROUP) if m not in WITH_Q]
    for m in range(GROUP):
        edges[m, :, :cols] = q_buf[:EDGE, mine[m]]
        edges[m, :, cols:] = q_buf[rows - EDGE :, mine[m]]
        if m in WITH_Q:
            at = pl.ds(rows + EDGE + tail_rows(m), half)
            for part in range(2):
                src = q_buf.at[pl.ds(part * half, half), mine[m]]
                store(src, kv_outs[m].at[at, pl.ds(part * cols, cols)])
        else:
            store(q_buf.at[:, mine[m]], q_outs[q_alone.index(m)])
    for m in TAILED:
        tails[m].wait()
        for part in range(2):
            at = pl.ds(rows + (1 + part) * EDGE, EDGE)
            store(tail.at[m, :, pl.ds(part * 2 * cols, 2 * cols)], kv_outs[m].at[at, :])
    for m in range(GROUP):
        store(edges.at[m], kv_outs[m].at[pl.ds(rows, EDGE), :])
    for copy in stores:
        copy.wait()


def split_columns(query, key, value, residual):
    rows, width = query.shape
    cols = width // GROUP
    kind = query.dtype
    dma = pltpu.SemaphoreType.DMA
    sizes = [
        rows + EDGE + tail_rows(m) + (rows // 2 if m in WITH_Q else 0) for m in range(GROUP)
    ]
    n_alone = GROUP - len(WITH_Q)
    got = pl.pallas_call(
        functools.partial(split_kernel, cols),
        out_shape=[jax.ShapeDtypeStruct((size, 2 * cols), kind) for size in sizes]
        + [jax.ShapeDtypeStruct((rows, cols), kind)] * n_alone,
        in_specs=[ANY] * 4,
        out_specs=[ANY] * (GROUP + n_alone),
        scratch_shapes=[
            pltpu.VMEM((rows, width), kind),
            pltpu.VMEM((2, rows, width), kind),
            pltpu.VMEM((GROUP, EDGE, 2 * cols), kind),
            pltpu.VMEM((GROUP, EDGE, width), kind),
            dma((6 + GROUP,)),
            dma((4 * GROUP + 2 * len(TAILED) + len(WITH_Q),)),
        ],
        compiler_params=pltpu.CompilerParams(vmem_limit_bytes=SPLIT_VMEM),
        name="split_columns",
    )(query, key, value, residual)
    return got[:GROUP], got[GROUP:]


def attend_kernel(rows, q_rows, widths, ms, q_at, lengths, *refs):
    ext = rows + 2 * EDGE
    kv_in, q_in, outs = refs[:KV_BLOCKS], refs[KV_BLOCKS : KV_BLOCKS + 2], refs[KV_BLOCKS + 2 : KV_BLOCKS + 4]
    q_buf, kv_buf, oh_buf, edges, ctx_buf, q_sem, kv_sem, edge_sem, out_sem, tail_sem, meta = refs[
        KV_BLOCKS + 4 :
    ]
    cols = q_buf.shape[1]
    half = rows // 2
    blocks = ctx_buf.shape[1] // q_rows
    _, base, which = group_place(rows)
    pair = which[ms[0]] // 2
    key_base = base + (2 * pair - 2) * rows
    place = [w - 2 * pair + 2 for w in which]
    place += [which[m] % 2 + 4 * pair for m in range(GROUP) if m not in ms]
    place += [which[m] % 2 for m in ms]
    copies = []
    for i, src in enumerate(kv_in):
        at = pl.multiple_of(place[i] * rows, 16)
        src_rows = src.at[pl.ds(0, rows), :]
        copies.append(pltpu.make_async_copy(src_rows, kv_buf.at[pl.ds(at, rows), :], kv_sem.at[i]))
        src_rows = src.at[pl.ds(rows, EDGE), :]
        copies.append(pltpu.make_async_copy(src_rows, edges.at[place[i]], edge_sem.at[i]))
    for i, src in enumerate(q_in):
        at = pl.multiple_of(place[KV_BLOCKS + i] * rows + EDGE, 16)
        if q_at[i] is None:
            dst = q_buf.at[pl.ds(at, rows), :]
            copies.append(pltpu.make_async_copy(src, dst, q_sem.at[2 * i]))
        else:
            for part in range(2):
                part_of = src.at[pl.ds(q_at[i], half), pl.ds(part * cols, cols)]
                dst = q_buf.at[pl.ds(at + part * half, half), :]
                copies.append(pltpu.make_async_copy(part_of, dst, q_sem.at[2 * i + part]))
    for copy in copies:
        copy.start()

    def hand_on(act):
        inner = (which[0] != 0) & (which[0] != GROUP - 1)
        for mine, src in ((inner, kv_in[0]), (jnp.logical_not(inner), kv_in[GROUP])):

            @pl.when(mine)
            def _(src=src):
                for i in range(4):
                    at = pl.ds(rows + (1 + i // 2) * EDGE, EDGE)
                    part = src.at[at, pl.ds(i % 2 * cols, cols)]
                    dst = outs[0].at[pl.ds(ext + i * EDGE, EDGE), :]
                    act(pltpu.make_async_copy(part, dst, tail_sem.at[i]))

    if GROUP - 1 in ms:
        hand_on(lambda copy: copy.start())

    utt_lane = lax.broadcasted_iota(jnp.int32, (1, oh_buf.shape[1]), 1)
    spans = []
    for m in ms:
        own = base + which[m] * rows
        spans += [(own, own + q_rows - EDGE - 1), (own + q_rows - EDGE, own + rows - 1)]

    def visit(u, carry):
        end, low_of, high_of, starts, ends = carry
        start, end = end, end + lengths[u]
        low_of = [jnp.where((a >= start) & (a < end), start, x) for (a, _), x in zip(spans, low_of)]
        high_of = [jnp.where((b >= start) & (b < end), end, x) for (_, b), x in zip(spans, high_of)]
        here = utt_lane == u
        return end, low_of, high_of, jnp.where(here, start, starts), jnp.where(here, end, ends)

    zero, none = jnp.int32(0), jnp.zeros(utt_lane.shape, jnp.int32)
    _, low_of, high_of, starts, ends = lax.fori_loop(
        0, lengths.shape[0], visit, (zero, [zero] * len(spans), [zero] * len(spans), none, none)
    )
    keys = kv_buf.shape[0]
    for t in range(len(spans)):
        low = jnp.maximum(low_of[t] - key_base, 0) // 16 * 16
        need = jnp.minimum(high_of[t] - key_base, keys) - low
        taken = widths[-1]
        for width in widths[-2::-1]:
            taken = jnp.where(need <= width, width, taken)
        meta[0, t] = jnp.minimum(low, keys - taken)
        meta[1, t] = need
        meta[2, t] = which[ms[t // blocks]] % 2 * rows + t % blocks * q_rows

    def one_hot(first, n, value):
        frame = first + lax.broadcasted_iota(jnp.int32, (n, utt_lane.shape[1]), 0)
        inside = (frame >= starts) & (frame < ends)
        return jnp.where(inside, jnp.float32(value), jnp.float32(0.0)).astype(jnp.bfloat16)

    @pl.loop(0, kv_buf.shape[0] // half)
    def _(i):
        at = pl.multiple_of(i * half, 16)
        oh_buf[pl.ds(at, half), :] = one_hot(key_base + at, half, 1.0)

    for copy in copies:
        copy.wait()
    q_buf[:EDGE, :] = edges[1, :, cols:]
    q_buf[EDGE + 2 * rows :, :] = edges[KV_BLOCKS - 2, :, :cols]

    lane = lax.broadcasted_iota(jnp.int32, (1, LANES), 1)
    scale = HD**-0.5
    halves = [
        jnp.where(lane // HD == h, jnp.float32(scale), jnp.float32(0.0)).astype(jnp.bfloat16)
        for h in range(2)
    ]

    def block(m, b, low, first, width):
        at = pl.multiple_of(b * q_rows, 16)
        oh_q = one_hot(key_base + 2 * rows - EDGE + first, q_rows, SAME)
        oh_k = oh_buf[pl.ds(low, width), :]
        oh_both = jnp.concatenate([oh_q, oh_q], axis=0)
        def scores(p_at):
            at_cols = slice(p_at, p_at + LANES)
            q = q_buf[pl.ds(first, q_rows), at_cols]
            k = jnp.concatenate([kv_buf[pl.ds(low, width), at_cols], oh_k], axis=1)
            q_both = jnp.concatenate([q * halves[0], q * halves[1]], axis=0)
            q_both = jnp.concatenate([q_both, oh_both], axis=1)
            return lax.dot_general(
                q_both, k, (((1,), (1,)), ((), ())), preferred_element_type=jnp.float32
            )

        def weigh(s, p_at):
            p = jnp.exp(s - jnp.max(s, axis=1, keepdims=True))
            return p.astype(jnp.bfloat16), jnp.sum(p, axis=1, keepdims=True)

        def combine(p, denom, p_at):
            v = kv_buf[pl.ds(low, width), cols + p_at : cols + p_at + LANES]
            o = jnp.dot(p, v, preferred_element_type=jnp.float32) / denom
            ctx = jnp.where(lane < HD, o[:q_rows], o[q_rows:])
            ctx_buf[m, pl.ds(at, q_rows), p_at : p_at + LANES] = ctx.astype(jnp.bfloat16)

        pairs = range(0, cols, LANES)
        got = [scores(p_at) for p_at in pairs]
        for p_at, s in zip(pairs, got):
            combine(*weigh(s, p_at), p_at)

    @pl.loop(0, 2 * blocks)
    def _(t):
        m, b = t // blocks, t % blocks
        low, need = pl.multiple_of(meta[0, t], 16), meta[1, t]
        first = pl.multiple_of(meta[2, t], 16)
        below = 0
        for width in widths:

            @pl.when((need > below) & (need <= width))
            def _(width=width):
                block(m, b, low, first, width)

            below = width

        for i in range(2):

            @pl.when(t == (i + 1) * blocks - 1)
            def _(i=i):
                dst = outs[i].at[pl.ds(0, ext), :]
                pltpu.make_async_copy(ctx_buf.at[i], dst, out_sem.at[i]).start()

    for i in range(2):
        dst = outs[i].at[pl.ds(0, ext), :]
        pltpu.make_async_copy(ctx_buf.at[i], dst, out_sem.at[i]).wait()
    if GROUP - 1 in ms:
        hand_on(lambda copy: copy.wait())


def attend(rows, cols, ms, q_at, lengths, kv_parts, q_parts):
    keys = KV_BLOCKS * rows
    ext = rows + 2 * EDGE
    q_rows = ext // 2
    most = -(-(q_rows + 4 * rows + 16) // LANES) * LANES
    widths = sorted({min(w, most) for w in WIDTHS + (most,)})
    utts = -(-lengths.shape[0] // LANES) * LANES
    shapes = [
        jax.ShapeDtypeStruct((ext + (4 * EDGE if m == GROUP - 1 else 0), cols), jnp.bfloat16)
        for m in ms
    ]
    dma = pltpu.SemaphoreType.DMA
    return pl.pallas_call(
        functools.partial(attend_kernel, rows, q_rows, widths, ms, q_at),
        out_shape=shapes,
        in_specs=[SMEM] + [ANY] * (KV_BLOCKS + 2),
        out_specs=[ANY] * 2,
        scratch_shapes=[
            pltpu.VMEM((2 * rows + 2 * EDGE, cols), jnp.bfloat16),
            pltpu.VMEM((keys, 2 * cols), jnp.bfloat16),
            pltpu.VMEM((keys, utts), jnp.bfloat16),
            pltpu.VMEM((KV_BLOCKS, EDGE, 2 * cols), jnp.bfloat16),
            pltpu.VMEM((2, ext, cols), jnp.bfloat16),
            dma((4,)),
            dma((KV_BLOCKS,)),
            dma((KV_BLOCKS,)),
            dma((2,)),
            dma((4,)),
            pltpu.SMEM((3, 4), jnp.int32),
        ],
        compiler_params=pltpu.CompilerParams(vmem_limit_bytes=ATTEND_VMEM),
        cost_estimate=pl.CostEstimate(
            flops=64 * ext * cols * keys, bytes_accessed=8 * keys * cols, transcendentals=0
        ),
        name="attend",
    )(lengths, *kv_parts, *q_parts)


def convolve(block_rows, ms, lengths, ctx_in, res, near_tail, other, kernel, mixed_out, conv_out, scratch):
    mixed, window, edges, starts, ends = scratch
    rows, width = res.shape
    _, base, which = group_place(rows)
    own = base + which[0] * rows
    per = width // LANES // GROUP
    taps = kernel.shape[0]
    half = taps // 2
    tiles = [
        (i, t, pl.ds(pl.multiple_of((which[m] * per + t) * LANES, LANES), LANES))
        for i, m in enumerate(ms)
        for t in range(per)
    ]

    def note(u, end):
        starts[u] = end
        ends[u] = end + lengths[u]
        return end + lengths[u]

    lax.fori_loop(0, lengths.shape[0], note, jnp.int32(0))
    side = which[0] % 2
    part = width // 2
    for i in range(2):
        edges[1 - side, :, i * part : (i + 1) * part] = near_tail[i * EDGE : (i + 1) * EDGE, :]
    part = width // 4
    for i in range(4):
        first = rows + (2 + i) * EDGE
        edges[side, :, i * part : (i + 1) * part] = other[first : first + EDGE, :]
    before, after = edges.at[0], edges.at[1]
    for slot, (i, t, cols) in enumerate(tiles):
        ctx = ctx_in[i][:, t * LANES : (t + 1) * LANES].astype(jnp.float32)
        for first, part in ((0, before), (EDGE, res), (EDGE + rows, after)):
            at = slice(first, first + part.shape[0])
            total = (part[:, cols].astype(jnp.float32) + ctx[at]).astype(jnp.bfloat16)
            mixed[slot, at, :] = total.astype(jnp.float32)
            if part is res:
                mixed_out[slot] = total

    span = block_rows + 2 * EDGE

    def past(frame):
        return lambda u: ends[u] <= frame

    @pl.loop(0, rows // block_rows, init_carry=jnp.int32(0))
    def _(b, first_utt):
        top = pl.multiple_of(b * block_rows, 16)
        around = own + top - EDGE + lax.broadcasted_iota(jnp.int32, (span, LANES), 0)
        frame = own + top + lax.broadcasted_iota(jnp.int32, (block_rows, LANES), 0)
        first_utt = lax.while_loop(past(own + top), lambda u: u + 1, first_utt)
        last_utt = lax.while_loop(past(own + top + block_rows - 1), lambda u: u + 1, first_utt)

        @pl.loop(first_utt, last_utt + 1)
        def _(u):
            low, high = starts[u], ends[u]
            kept = (around >= low) & (around < high)
            mine = (frame >= low) & (frame < high)
            for slot in range(len(tiles)):
                window[slot] = jnp.where(kept, mixed[slot, pl.ds(top, span), :], jnp.float32(0.0))
            for slot, (_, _, cols) in enumerate(tiles):
                total = jnp.zeros((block_rows, LANES), jnp.float32)
                for tap in range(taps):
                    at = tap + EDGE - half
                    total = total + window[slot, at : at + block_rows, :] * kernel[tap : tap + 1, cols]
                at = pl.ds(top, block_rows)
                conv_out[slot, at, :] = jnp.where(mine, total, conv_out[slot, at, :])

        return last_utt


def convolve_kernel(block_rows, ms, lengths, *refs):
    ctx_in = refs[: len(ms)]
    res, near_tail, other, kernel, mixed_out, conv_out = refs[len(ms) : len(ms) + 6]
    scratch = refs[len(ms) + 6 :]
    convolve(block_rows, ms, lengths, ctx_in, res, near_tail, other, kernel, mixed_out, conv_out, scratch)


def finish_kernel(block_rows, ms, early, lengths, *refs):
    ctx_in = refs[: len(ms)]
    res, near_tail, other, kernel, gain, shift, mixed_in, conv_in, out = refs[len(ms) : len(ms) + 9]
    mixed_own, conv_own = refs[len(ms) + 9 : len(ms) + 11]
    scratch = refs[len(ms) + 11 :]
    convolve(block_rows, ms, lengths, ctx_in, res, near_tail, other, kernel, mixed_own, conv_own, scratch)
    rows, width = res.shape
    _, _, which = group_place(rows)
    per = width // LANES // GROUP
    sources = []
    for group, mixed, conv in ((early, mixed_in, conv_in), (ms, mixed_own, conv_own)):
        for i, m in enumerate(group):
            for t in range(per):
                cols = pl.ds(pl.multiple_of((which[m] * per + t) * LANES, LANES), LANES)
                sources.append((mixed, conv, i * per + t, cols))

    norm_rows = rows // 2

    @pl.loop(0, 2)
    def _(b):
        at = pl.ds(pl.multiple_of(b * norm_rows, 16), norm_rows)
        values = [conv[slot, at, :] for _, conv, slot, _ in sources]
        mean = jnp.sum(sum(values), axis=1, keepdims=True) / width
        centred = [x - mean for x in values]
        var = jnp.sum(sum([x * x for x in centred]), axis=1, keepdims=True) / width
        inverse = 1.0 / jnp.sqrt(var + 1e-05)
        for x, (mixed, _, slot, cols) in zip(centred, sources):
            normed = x * inverse * gain[:, cols] + shift[:, cols]
            gated = 0.5 * normed * (1.0 + jnp.tanh(0.5 * normed))
            out[at, cols] = (mixed[slot, at, :].astype(jnp.float32) + gated).astype(jnp.bfloat16)


def conv_scratch(slots, rows, width, block_rows, utts):
    return [
        pltpu.VMEM((slots, rows + 2 * EDGE, LANES), jnp.float32),
        pltpu.VMEM((slots, block_rows + 2 * EDGE, LANES), jnp.float32),
        pltpu.VMEM((2, EDGE, width), jnp.bfloat16),
        pltpu.SMEM((utts,), jnp.int32),
        pltpu.SMEM((utts,), jnp.int32),
    ]


def convolve_early(ms, lengths, ctx_parts, res, near_tail, other, kernel):
    rows, width = res.shape
    slots = len(ms) * width // LANES // GROUP
    taps = kernel.shape[0]
    return pl.pallas_call(
        functools.partial(convolve_kernel, BLOCK_ROWS, ms),
        out_shape=[
            jax.ShapeDtypeStruct((slots, rows, LANES), jnp.bfloat16),
            jax.ShapeDtypeStruct((slots, rows, LANES), jnp.float32),
        ],
        in_specs=[SMEM] + [VMEM] * (len(ms) + 4),
        out_specs=[VMEM] * 2,
        scratch_shapes=conv_scratch(slots, rows, width, BLOCK_ROWS, lengths.shape[0]),
        compiler_params=pltpu.CompilerParams(vmem_limit_bytes=FINISH_VMEM),
        cost_estimate=pl.CostEstimate(
            flops=100 * taps * rows * slots * LANES, bytes_accessed=8 * rows * width, transcendentals=0
        ),
        name="convolve",
    )(lengths, *ctx_parts, res, near_tail, other, kernel)


def finish(ms, early, lengths, ctx_parts, res, near_tail, other, kernel, gain, shift, mixed, conv):
    rows, width = res.shape
    slots = len(ms) * width // LANES // GROUP
    return pl.pallas_call(
        functools.partial(finish_kernel, BLOCK_ROWS, ms, early),
        out_shape=jax.ShapeDtypeStruct((rows, width), jnp.bfloat16),
        in_specs=[SMEM] + [VMEM] * (len(ms) + 8),
        out_specs=VMEM,
        scratch_shapes=[
            pltpu.VMEM((slots, rows, LANES), jnp.bfloat16),
            pltpu.VMEM((slots, rows, LANES), jnp.float32),
        ]
        + conv_scratch(slots, rows, width, BLOCK_ROWS, lengths.shape[0]),
        compiler_params=pltpu.CompilerParams(vmem_limit_bytes=FINISH_VMEM),
        name="finish",
    )(lengths, *ctx_parts, res, near_tail, other, kernel, gain, shift, mixed, conv)


def local(query, key, value, residual, lengths, depth_kernel, gain, shift):
    rows, width = query.shape
    cols = width // GROUP
    peers = lax.axis_size("seq")

    def swap(array, m):
        return lax.ppermute(array, "seq", [(i, i ^ m) for i in range(peers)])

    def move(array, by):
        pairs = [(i, i + by(i)) for i in range(peers)]
        return lax.ppermute(array, "seq", [(i, j) for i, j in pairs if 0 <= j < peers])

    near = lambda i: -GROUP if i % GROUP < GROUP // 2 else GROUP
    far = lambda i: -near(i)

    kv, q_alone = split_columns(query, key, value, residual)
    kv_group = [kv[0]] + [swap(kv[m], m) for m in range(1, GROUP)]
    q_2, q_3, kv_group[1] = lax.optimization_barrier((*q_alone[2:], kv_group[1]))
    q_3, q_2 = swap(q_3, 3), swap(q_2, 2)
    q_1, kv_group[3] = lax.optimization_barrier((q_alone[1], kv_group[3]))
    q_near = [swap(q_1, 1), q_alone[0]]
    bare = [part[: rows + EDGE + tail_rows(m)] for m, part in enumerate(kv_group)]
    kv_halo = [move(bare[m], near) for m in range(2)]
    both = move(jnp.concatenate(bare[2:], axis=0), far)
    kv_halo += [both[: bare[2].shape[0]], both[bare[2].shape[0] :]]

    q_at = (None, None)
    far_q = [q_3, q_2]
    ctx_far = attend(rows, cols, (3, 2), q_at, lengths, kv_group + kv_halo[:2], far_q)
    ctx_3, ctx_2 = swap(ctx_far[0], 3), swap(ctx_far[1], 2)
    ctx_near = attend(rows, cols, (1, 0), (None, None), lengths, kv_group + kv_halo[2:], q_near)
    ctx_1 = swap(ctx_near[0], 1)

    near_tail = kv_group[1][rows + EDGE : rows + 3 * EDGE]
    around = (residual, near_tail, ctx_3, depth_kernel)
    early = (0, 2, 3)
    mixed, conv = convolve_early(early, lengths, [ctx_near[1], ctx_2, ctx_3], *around)
    late = (1,)
    return finish(late, early, lengths, [ctx_1], *around, gain[None, :], shift[None, :], mixed, conv)


def solution(mesh):
    return jax.shard_map(
        local,
        mesh=mesh,
        in_specs=(
            P(("dp", "seq"), None),
            P(("dp", "seq"), None),
            P(("dp", "seq"), None),
            P(("dp", "seq"), None),
            P("dp"),
            P(),
            P(),
            P(),
        ),
        out_specs=P(("dp", "seq"), None),
        check_vma=False,
    )
```
